32 devices in a mesh: groups: 2 (over x), ffn: 16 (over z, y, core).
Axes of the slice: x: 2, y: 2, z: 4, core: 2. Of those that a mesh axis runs over, the one named last changes fastest.
Arguments:
- queries: bfloat16 [32, 2, 32, 1024], P(('groups', 'ffn')), parts along dimension 0, may hold values from -100 to 100
- block_kv: bfloat16 [32, 2, 32, 256], P(('groups', 'ffn')), parts along dimension 0, may hold values from -4 to 4
- cache_kv: bfloat16 [32, 2, 1536, 256], P(('groups', 'ffn')), parts along dimension 0, may hold values from -6 to 6
- prefix_len: int32 [8], P('groups'), parts along dimension 0, may hold values from 1 to 1536, as said below
- block_valid: int32 [8], P('groups'), parts along dimension 0, may hold values from 16 to 32, as said below
- resid: bfloat16 [32, 2, 32, 1024], P(('groups', 'ffn')), parts along dimension 0, may hold values from -6 to 6
- norm_gain: float32 [8192], replicated, may hold values from 0.25 to 1.75
- w_gate: bfloat16 [8192, 14336], P(None, 'ffn'), may hold values from -0.0625 to 0.0625
- w_up: bfloat16 [8192, 14336], P(None, 'ffn'), may hold values from -0.0625 to 0.0625
- w_down: bfloat16 [14336, 8192], P('ffn'), may hold values from -0.0625 to 0.0625
Outputs:
- layer_out: bfloat16 [32, 2, 32, 1024], P(('groups', 'ffn')), parts along dimension 0
The draws below stay inside these ranges and needn't reach their ends.
There are 2 independent parts, one for each index of `groups`. The reference program is written for one: setup_inputs(seed, part) draws one part's arguments, and reference() takes and returns one part's arrays. A program takes and returns all parts, laid end to end along the dimension named above; an argument that names none is the same for every part. Nothing has to cross between parts.
Inputs may be any that keep to these rules, and one draw needn't show every extreme that they name: `prefix_len`: some request has exactly 1536. `block_valid`: some request has exactly 32.
All inputs are finite; a program needn't handle non-finite values.
Results may differ from the reference program's by a relative error of at most 0.0061.
Values may be sent and summed in bfloat16 or wider, within the bound.
A program may use at most 128 MiB of HBM per device.

```python
import jax
import jax.numpy as jnp
from jax import lax

KVH = 8
GQA = 8
HD = 128
FF = 14336
BLK = 32
LMAX = 1536
REQ_DEV = 2
D = 8192
SLOTS = 16
RGROUPS = 2
REQ = 4
TOKENS = 128


def joint_blocks(key):
    base_key = jax.random.fold_in(key, 11)
    query_key, block_key = jax.random.split(base_key)
    query_draw = jnp.clip(jax.random.normal(query_key, (SLOTS, REQ_DEV, BLK, GQA * HD), jnp.float32), -4.0, 4.0)
    block_draw = jnp.clip(jax.random.normal(block_key, (SLOTS, REQ_DEV, BLK, 2 * HD), jnp.float32), -4.0, 4.0)
    return (query_draw, block_draw)


def draw_queries(key, part):
    return joint_blocks(key)[0].astype(jnp.bfloat16)


def draw_block_kv(key, part):
    return joint_blocks(key)[1].astype(jnp.bfloat16)


def draw_prefix_len(key, part):
    first_key, second_key = jax.random.split(jax.random.fold_in(key, 23))
    lengths = jax.random.randint(first_key, (REQ,), 1, LMAX + 1).astype(jnp.int32)
    chosen = jax.random.randint(second_key, (), 0, REQ)
    return lengths.at[chosen].set(LMAX).astype(jnp.int32)


def draw_block_valid(key, part):
    first_key, second_key = jax.random.split(jax.random.fold_in(key, 37))
    counts = jax.random.randint(first_key, (REQ,), BLK // 2, BLK + 1).astype(jnp.int32)
    lower = jax.random.randint(second_key, (), BLK // 2, BLK).astype(jnp.int32)
    part_value = jnp.asarray(part, jnp.int32)
    full_index = jnp.asarray(part_value % REQ, jnp.int32)
    short_index = jnp.asarray((part_value + 1) % REQ, jnp.int32)
    counts = counts.at[short_index].set(lower)
    return counts.at[full_index].set(BLK).astype(jnp.int32)


def with_spikes(values, stream_key, source, target, shards_of, factor):
    def block_of(position):
        return (jnp.arange(values.shape[position]) // (values.shape[position] // shards_of)).reshape((-1,) + (1,) * (values.ndim - 1 - position))

    one_side = jax.random.permutation(stream_key, shards_of)[block_of(target)]
    second = (block_of(target) + shards_of // 2) % shards_of
    return jnp.where((block_of(source) == one_side) | (block_of(source) == second), factor * values, values)


def level_of(rng, extent, pieces, low, largest):
    loudness, own = 1.0, jax.random.fold_in(rng, 6)
    for axis_at, parts in pieces:
        heights = jnp.exp(jax.random.uniform(jax.random.fold_in(own, axis_at), (parts,), jnp.float32, low / len(pieces), largest / len(pieces)))
        loudness = loudness * jnp.repeat(heights, extent[axis_at] // parts).reshape([-1 if axis == axis_at else 1 for axis in range(len(extent))])
    return loudness


def scatter_about(rng, shape, scale, most, pieces=(), kind=jnp.bfloat16):
    result = scale * jax.random.normal(rng, shape, jnp.float32)
    if pieces:
        result = result * level_of(rng, shape, pieces, -0.22, 0.18)
    return jnp.clip(result, -most, most).astype(kind)


def bell_draw_with(key, extent, scale, reach, cuts, heavy, kind=jnp.bfloat16):
    drawn = scale * jax.random.normal(key, extent, jnp.float32)
    if cuts:
        drawn = drawn * level_of(key, extent, cuts, -0.22, 0.18)
    return jnp.clip(with_spikes(drawn, jax.random.fold_in(key, 3), *heavy), -reach, reach).astype(kind)


def setup_inputs(seed: int = 0, part: int = 0) -> dict:
    key_of = jax.random.split(jax.random.key(seed), 11)
    part_splits = jax.random.split(jax.random.fold_in(key_of[10], part), 11)
    queries = draw_queries(jax.random.fold_in(jax.random.fold_in(key_of[10], part), 71), part)
    block_kv = draw_block_kv(jax.random.fold_in(jax.random.fold_in(key_of[10], part), 71), part)
    cache_kv = scatter_about(part_splits[2], (SLOTS, REQ_DEV, LMAX, 2 * HD), 1.0, 6.0, ((0, 16),))
    prefix_len = draw_prefix_len(jax.random.fold_in(jax.random.fold_in(key_of[10], part), 71), part)
    block_valid = draw_block_valid(jax.random.fold_in(jax.random.fold_in(key_of[10], part), 71), part)
    resid = scatter_about(part_splits[5], (SLOTS, REQ_DEV, BLK, GQA * HD), 1.0, 6.0, ((0, 16),))
    norm_gain = jnp.clip(1.0 + 0.15 * jax.random.normal(key_of[6], (D,), jnp.float32), 0.25, 1.75)
    w_gate = scatter_about(key_of[7], (D, FF), D ** -0.5, 0.0625, ((1, 16),))
    w_up = scatter_about(key_of[8], (D, FF), D ** -0.5, 0.0625, ((1, 16),))
    w_down = bell_draw_with(key_of[9], (FF, D), FF ** -0.5, 0.0625, ((0, 16),), (0, 1, 16, 2.0))
    return dict(queries=queries, block_kv=block_kv, cache_kv=cache_kv, prefix_len=prefix_len, block_valid=block_valid, resid=resid, norm_gain=norm_gain, w_gate=w_gate, w_up=w_up, w_down=w_down)


def attend_all(queries, block_kv, cache_kv, prefix_here, valid_here):
    slot_count = queries.shape[0]
    keys_all = jnp.concatenate([cache_kv[..., :HD], block_kv[..., :HD]], axis=2).astype(jnp.float32)
    values_all = jnp.concatenate([cache_kv[..., HD:], block_kv[..., HD:]], axis=2).astype(jnp.float32)
    positions = jnp.arange(LMAX + BLK)
    visible = jnp.where(positions[None, None, :] < LMAX, positions[None, None, :] < prefix_here[:, :, None], positions[None, None, :] - LMAX < valid_here[:, :, None])
    query_heads = queries.astype(jnp.float32).reshape(slot_count, REQ_DEV, BLK, GQA, HD)
    scores = jnp.einsum('srbgd,srkd->srgbk', query_heads, keys_all) * (1.0 / jnp.sqrt(jnp.float32(HD)))
    masked = jnp.where(visible[:, :, None, None, :], scores, jnp.float32(-1e+30))
    peak = lax.optimization_barrier(jnp.max(masked, axis=-1, keepdims=True))
    exps = jnp.exp(masked - peak)
    totals = lax.optimization_barrier(jnp.sum(exps, axis=-1, keepdims=True))
    probability = (exps / totals).astype(jnp.bfloat16)
    mixed = jnp.einsum('srgbk,srkd->srbgd', probability.astype(jnp.float32), values_all)
    return mixed.reshape(slot_count, REQ_DEV, BLK, GQA * HD)

def reference(queries, block_kv, cache_kv, prefix_len, block_valid, resid, norm_gain, w_gate, w_up, w_down):
    width = GQA * HD
    slot_request = ((jnp.arange(SLOTS) // KVH)[:, None] * REQ_DEV + jnp.arange(REQ_DEV)[None, :]).astype(jnp.int32)
    prefix_here = prefix_len[slot_request]
    valid_here = block_valid[slot_request]
    attended = attend_all(queries, block_kv, cache_kv, prefix_here, valid_here)
    mid_state = (resid.astype(jnp.float32) + attended).astype(jnp.bfloat16)
    mid_split = mid_state.astype(jnp.float32).reshape(RGROUPS, KVH, REQ_DEV, BLK, width)
    mean_square = lax.optimization_barrier(jnp.sum(mid_split * mid_split, axis=(1, 4))) / D
    inv_root = lax.rsqrt(mean_square + 1e-05)
    gain_split = norm_gain.reshape(KVH, width)[None, :, None, None, :]
    normed = (mid_split * inv_root[:, None, :, :, None] * gain_split).astype(jnp.bfloat16)
    token_rows = jnp.transpose(normed, (0, 2, 3, 1, 4)).reshape(TOKENS, D)
    gate_proj = jnp.dot(token_rows, w_gate, preferred_element_type=jnp.float32)
    up_proj = jnp.dot(token_rows, w_up, preferred_element_type=jnp.float32)
    hidden = (jax.nn.silu(gate_proj) * up_proj).astype(jnp.bfloat16)
    ffn_sum = jnp.dot(hidden, w_down, preferred_element_type=jnp.float32)
    ffn_split = jnp.transpose(ffn_sum.reshape(RGROUPS, REQ_DEV, BLK, KVH, width), (0, 3, 1, 2, 4))
    ffn_split = ffn_split.reshape(SLOTS, REQ_DEV, BLK, width)
    return (mid_state.astype(jnp.float32) + ffn_split).astype(jnp.bfloat16)
```

```python
import functools

import jax
import jax.numpy as jnp
from jax import lax
from jax.experimental import pallas as pl
from jax.experimental.pallas import tpu as pltpu
from jax.sharding import PartitionSpec as P

KVH = 8
CORES = 2

epsilon = 1e-05


def ring_is_snake(mesh):
    row = mesh.devices.reshape(mesh.shape["groups"], mesh.shape["ffn"])[0]
    chips = [getattr(row[i], "coords", None) for i in range(0, len(row), CORES)]
    if len(chips) < 4 or any(c is None for c in chips):
        return False
    return any(
        all(c[axis] == chips[i % 2][axis] for i, c in enumerate(chips))
        and chips[0][axis] != chips[1][axis]
        for axis in range(len(chips[0]))
    )


def layer_kernel(
    ring,
    snake,
    q_ref,
    bkv_ref,
    cache_hbm,
    prefix_ref,
    valid_ref,
    resid_ref,
    gain_ref,
    wg_hbm,
    wu_hbm,
    wd_hbm,
    out_ref,
    cache,
    wg,
    wu,
    wd,
    xg,
    acc_g,
    acc_u,
    sumsq,
    hid,
    csum,
    psend,
    precv,
    rsend,
    rrecv,
    lsend,
    lrecv,
    cache_sem,
    w_sem,
    ag_recv,
    ag_right,
    ag_left,
    ag_pair,
    p_ssem,
    p_rsem,
    r_ssem,
    r_rsem,
    l_ssem,
    l_rsem,
):
    reqs, block_len, width = q_ref.shape
    cache_len = cache.shape[1]
    head_size = cache.shape[2] // 2
    heads = width // head_size
    hidden_here = wg.shape[1]
    model_width = KVH * width
    groups = acc_g.shape[0]
    rows = reqs * block_len
    pairs = KVH // CORES
    half = ring // 2
    me = lax.axis_index("ffn")
    core = me % CORES
    chip = me // CORES
    if snake:
        here = (1 - chip % 2) * (chip // 2) + (chip % 2) * (ring - 1 - chip // 2)
    else:
        here = chip

    def chip_at(offset):
        place = (here + offset + ring) % ring
        if not snake:
            return place
        back = place // half
        return (1 - back) * (2 * place) + back * (2 * (ring - 1 - place) + 1)

    partner = chip * CORES + (1 - core)
    right = chip_at(1) * CORES + core
    left = chip_at(-1) * CORES + core

    barrier = pltpu.get_barrier_semaphore()
    for other in (partner, right, left):
        pl.semaphore_signal(
            barrier, inc=1, device_id={"ffn": other}, device_id_type=pl.DeviceIdType.MESH
        )

    cache_copies = [
        pltpu.make_async_copy(cache_hbm.at[r], cache.at[r], cache_sem.at[r]) for r in range(reqs)
    ]
    for copy in cache_copies:
        copy.start()
    weight_copies = []
    for w, (source, target) in enumerate(((wg_hbm, wg), (wu_hbm, wu))):
        for h in range(KVH):
            span = pl.ds(h * width, width)
            weight_copies.append(
                pltpu.make_async_copy(source.at[span], target.at[span], w_sem.at[w, h])
            )
    down_copies = []
    for h in range(KVH):
        span = pl.ds(h * width, width)
        down_copies.append(
            pltpu.make_async_copy(wd_hbm.at[:, span], wd.at[:, span], w_sem.at[2, h])
        )
    for copy in weight_copies + down_copies:
        copy.start()

    def send(source, target, ssem, rsem, device):
        return pltpu.make_async_remote_copy(
            src_ref=source,
            dst_ref=target,
            send_sem=ssem,
            recv_sem=rsem,
            device_id={"ffn": device},
            device_id_type=pl.DeviceIdType.MESH,
        )

    def to_right(s, i):
        return send(xg.at[s, i], xg.at[s, i], ag_right.at[s, i], ag_recv.at[s, i], right)

    def to_left(s, i):
        return send(xg.at[s, i], xg.at[s, i], ag_left.at[s, i], ag_recv.at[s, i], left)

    def to_pair(s, i):
        return send(xg.at[s, i], xg.at[s, i], ag_pair.at[s, i], ag_recv.at[s, i], partner)

    def goes_right(i):
        return i < reqs // 2

    group = me // KVH
    scale = 1.0 / (head_size**0.5)
    for r in range(reqs):
        cache_copies[r].wait()
        query = q_ref[r]
        stacked = jnp.concatenate(
            [query[:, h * head_size : (h + 1) * head_size] for h in range(heads)], axis=0
        )
        contract = (((1,), (1,)), ((), ()))
        far = lax.dot_general(
            stacked, cache[r, :, :head_size], contract, preferred_element_type=jnp.float32
        )
        near = lax.dot_general(
            stacked, bkv_ref[r, :, :head_size], contract, preferred_element_type=jnp.float32
        )
        seen = prefix_ref[group * reqs + r]
        live = valid_ref[group * reqs + r]
        far_at = lax.broadcasted_iota(jnp.int32, (1, cache_len), 1)
        near_at = lax.broadcasted_iota(jnp.int32, (1, block_len), 1)
        far = jnp.where(far_at < seen, far * scale, -1e30)
        near = jnp.where(near_at < live, near * scale, -1e30)
        peak = jnp.maximum(
            jnp.max(far, axis=-1, keepdims=True), jnp.max(near, axis=-1, keepdims=True)
        )
        far = jnp.exp(far - peak)
        near = jnp.exp(near - peak)
        total = jnp.sum(far, axis=-1, keepdims=True) + jnp.sum(near, axis=-1, keepdims=True)
        inverse = 1.0 / total
        mixed = jnp.dot(
            (far * inverse).astype(jnp.bfloat16),
            cache[r, :, head_size:],
            preferred_element_type=jnp.float32,
        ) + jnp.dot(
            (near * inverse).astype(jnp.bfloat16),
            bkv_ref[r, :, head_size:],
            preferred_element_type=jnp.float32,
        )
        side = jnp.concatenate(
            [mixed[h * block_len : (h + 1) * block_len] for h in range(heads)], axis=1
        )
        xg[me, r] = (resid_ref[r].astype(jnp.float32) + side).astype(jnp.bfloat16)
        if r == 0:
            pl.semaphore_wait(barrier, 3)
        to_right(me, r).start()
        to_left(me, r).start()
        to_pair(me, r).start()

    acc_g[...] = jnp.zeros_like(acc_g)
    acc_u[...] = jnp.zeros_like(acc_u)
    sumsq[...] = jnp.zeros_like(sumsq)

    def absorb(s):
        g = s // KVH
        span = pl.ds(pl.multiple_of((s % KVH) * width, width), width)
        block = xg[s].reshape(rows, width).astype(jnp.float32)
        square = block * block
        folded = square[:, :head_size]
        for h in range(1, heads):
            folded = folded + square[:, h * head_size : (h + 1) * head_size]
        sumsq[g] += folded
        scaled = (block * gain_ref[:, span]).astype(jnp.bfloat16)
        acc_g[g] += jnp.dot(scaled, wg[span, :], preferred_element_type=jnp.float32)
        acc_u[g] += jnp.dot(scaled, wu[span, :], preferred_element_type=jnp.float32)

    def absorb_pair(s):
        for i in range(reqs):
            to_pair(s, i).wait_recv()
        absorb(s)

    def pass_on(t, last):
        from_left = chip_at(-t) * CORES + core
        from_right = chip_at(t) * CORES + core
        for i in range(reqs):
            to_right(from_left, i).wait_recv()
            if not last or goes_right(i):
                to_right(from_left, i).start()
            to_pair(from_left, i).start()
            to_left(from_right, i).wait_recv()
            if not last or not goes_right(i):
                to_left(from_right, i).start()
            to_pair(from_right, i).start()

    def absorb_step(t):
        absorb(chip_at(-t) * CORES + core)
        absorb(chip_at(t) * CORES + core)
        absorb_pair(chip_at(-t) * CORES + 1 - core)
        absorb_pair(chip_at(t) * CORES + 1 - core)

    pass_on(1, half == 2)
    for copy in weight_copies:
        copy.wait()
    absorb(me)
    absorb_pair(partner)
    absorb_step(1)

    def middle(t, carry):
        pass_on(t, False)
        absorb_step(t)
        return carry

    if half > 2:
        lax.fori_loop(2, half - 1, middle, 0)
        pass_on(half - 1, True)
        absorb_step(half - 1)
    far_chip = chip_at(half)
    for i in range(reqs):
        (to_right if goes_right(i) else to_left)(far_chip * CORES + core, i).wait_recv()
        to_pair(far_chip * CORES + core, i).start()
    absorb(far_chip * CORES + core)
    absorb_pair(far_chip * CORES + 1 - core)

    for g in range(groups):
        mean_square = jnp.sum(sumsq[g], axis=-1, keepdims=True) / model_width
        root = lax.rsqrt(mean_square + epsilon)
        gate = acc_g[g] * root
        up = acc_u[g] * root
        hid[g * rows : (g + 1) * rows, :] = (gate * jax.nn.sigmoid(gate) * up).astype(jnp.bfloat16)

    for copy in down_copies:
        copy.wait()

    def pair_copy(k):
        return send(psend.at[k], precv.at[k], p_ssem.at[k], p_rsem.at[k], partner)

    def column_of(k, parity):
        return pl.ds(pl.multiple_of((k * CORES + parity) * width, width), width)

    def give(j, carry):
        k = (far_chip + j) % pairs
        share = jnp.dot(
            hid[...], wd[:, column_of(k, 1 - core)], preferred_element_type=jnp.float32
        )
        psend[k] = share.astype(jnp.bfloat16).reshape(groups, reqs, block_len, width)
        pair_copy(k).start()
        return carry

    def keep(j, carry):
        k = (far_chip + j) % pairs
        share = jnp.dot(hid[...], wd[:, column_of(k, core)], preferred_element_type=jnp.float32)
        pair_copy(k).wait_recv()
        csum[k] = share.reshape(groups, reqs, block_len, width) + precv[k].astype(jnp.float32)
        return carry

    lax.fori_loop(0, pairs, give, 0)
    lax.fori_loop(0, pairs, keep, 0)

    def right_copy(t, i):
        return send(rsend.at[t, i], rrecv.at[t, i], r_ssem.at[t, i], r_rsem.at[t, i], right)

    def left_copy(t, i):
        return send(lsend.at[t, i], lrecv.at[t, i], l_ssem.at[t, i], l_rsem.at[t, i], left)

    sent = []
    for t in range(half, 0, -1):
        for i in range(reqs):
            for copy_of, out_buf, in_buf, offset, first in (
                (right_copy, rsend, rrecv, t, goes_right(i)),
                (left_copy, lsend, lrecv, -t, not goes_right(i)),
            ):
                if t == half and not first:
                    continue
                target = chip_at(offset)
                value = csum[target % pairs, target // pairs, i]
                if t < half - 1 or (t == half - 1 and first):
                    copy_of(t, i).wait_recv()
                    value = value + in_buf[t, i].astype(jnp.float32)
                out_buf[t - 1, i] = value.astype(jnp.bfloat16)
                copy_of(t - 1, i).start()
                sent.append(copy_of(t - 1, i))
    for i in range(reqs):
        right_copy(0, i).wait_recv()
        left_copy(0, i).wait_recv()
        value = csum[chip % pairs, chip // pairs, i]
        value = value + rrecv[0, i].astype(jnp.float32) + lrecv[0, i].astype(jnp.float32)
        out_ref[i] = (xg[me, i].astype(jnp.float32) + value).astype(jnp.bfloat16)

    for copy in sent:
        copy.wait_send()

    def pair_sent(k, carry):
        pair_copy(k).wait_send()
        return carry

    lax.fori_loop(0, pairs, pair_sent, 0)

    def gather_sent(t, carry):
        for i in range(reqs):
            to_right(chip_at(-t) * CORES + core, i).wait_send()
            to_pair(chip_at(-t) * CORES + core, i).wait_send()
            to_left(chip_at(t) * CORES + core, i).wait_send()
            to_pair(chip_at(t) * CORES + core, i).wait_send()
        return carry

    for i in range(reqs):
        to_right(me, i).wait_send()
        to_left(me, i).wait_send()
        to_pair(me, i).wait_send()
        to_pair(far_chip * CORES + core, i).wait_send()
        (to_right(chip_at(1 - half) * CORES + core, i) if goes_right(i) else to_left(
            chip_at(half - 1) * CORES + core, i
        )).wait_send()
        to_pair(chip_at(1 - half) * CORES + core, i).wait_send()
        to_pair(chip_at(half - 1) * CORES + core, i).wait_send()
    lax.fori_loop(1, half - 1, gather_sent, 0)


def body(
    snake,
    queries,
    block_kv,
    cache_kv,
    prefix_len,
    block_valid,
    resid,
    norm_gain,
    w_gate,
    w_up,
    w_down,
):
    count = lax.axis_size("ffn")
    ring = count // CORES
    half = ring // 2
    _, reqs, block_len, width = queries.shape
    hidden_here = w_gate.shape[1]
    groups = count // KVH
    rows = reqs * block_len
    pairs = KVH // CORES
    lanes = block_kv.shape[3] // 2
    bf16, f32 = jnp.bfloat16, jnp.float32
    vmem = pl.BlockSpec(memory_space=pltpu.VMEM)
    smem = pl.BlockSpec(memory_space=pltpu.SMEM)
    hbm = pl.BlockSpec(memory_space=pl.ANY)
    dma = pltpu.SemaphoreType.DMA
    flops = 2 * groups * rows * KVH * width * hidden_here * 3
    out = pl.pallas_call(
        functools.partial(layer_kernel, ring, snake),
        out_shape=jax.ShapeDtypeStruct((reqs, block_len, width), bf16),
        in_specs=[vmem, vmem, hbm, smem, smem, vmem, vmem, hbm, hbm, hbm],
        out_specs=vmem,
        scratch_shapes=[
            pltpu.VMEM(cache_kv.shape[1:], bf16),
            pltpu.VMEM(w_gate.shape, bf16),
            pltpu.VMEM(w_up.shape, bf16),
            pltpu.VMEM(w_down.shape, bf16),
            pltpu.VMEM((count, reqs, block_len, width), bf16),
            pltpu.VMEM((groups, rows, hidden_here), f32),
            pltpu.VMEM((groups, rows, hidden_here), f32),
            pltpu.VMEM((groups, rows, lanes), f32),
            pltpu.VMEM((groups * rows, hidden_here), bf16),
            pltpu.VMEM((pairs, groups, reqs, block_len, width), f32),
            pltpu.VMEM((pairs, groups, reqs, block_len, width), bf16),
            pltpu.VMEM((pairs, groups, reqs, block_len, width), bf16),
            pltpu.VMEM((half, reqs, block_len, width), bf16),
            pltpu.VMEM((half, reqs, block_len, width), bf16),
            pltpu.VMEM((half, reqs, block_len, width), bf16),
            pltpu.VMEM((half, reqs, block_len, width), bf16),
            dma((reqs,)),
            dma((3, KVH)),
            dma((count, reqs)),
            dma((count, reqs)),
            dma((count, reqs)),
            dma((count, reqs)),
            dma((pairs,)),
            dma((pairs,)),
            dma((half, reqs)),
            dma((half, reqs)),
            dma((half, reqs)),
            dma((half, reqs)),
        ],
        compiler_params=pltpu.CompilerParams(
            collective_id=0, has_side_effects=True, vmem_limit_bytes=62 * 1024 * 1024
        ),
        cost_estimate=pl.CostEstimate(
            flops=flops, bytes_accessed=6 * KVH * width * hidden_here, transcendentals=0
        ),
    )(
        queries[0],
        block_kv[0],
        cache_kv[0],
        prefix_len,
        block_valid,
        resid[0],
        norm_gain.reshape(1, -1),
        w_gate,
        w_up,
        w_down,
    )
    return out[None]


def solution(mesh):
    in_specs = (
        P(("groups", "ffn"), None, None, None),
        P(("groups", "ffn"), None, None, None),
        P(("groups", "ffn"), None, None, None),
        P("groups"),
        P("groups"),
        P(("groups", "ffn"), None, None, None),
        P(),
        P(None, "ffn"),
        P(None, "ffn"),
        P("ffn", None),
    )
    out_specs = P(("groups", "ffn"), None, None, None)
    return jax.shard_map(
        functools.partial(body, ring_is_snake(mesh)),
        mesh=mesh,
        in_specs=in_specs,
        out_specs=out_specs,
        check_vma=False,
    )
```

```python
import functools
import math

import jax
import jax.numpy as jnp
from jax import lax
from jax.experimental import pallas as pl
from jax.experimental.pallas import tpu as pltpu
from jax.sharding import PartitionSpec as P

KVH = 8
CORES = 2

epsilon = 1e-05


def ring_is_snake(mesh):
    row = mesh.devices.reshape(mesh.shape["groups"], mesh.shape["ffn"])[0]
    chips = [getattr(row[i], "coords", None) for i in range(0, len(row), CORES)]
    if len(chips) < 4 or any(c is None for c in chips):
        return False
    return any(
        all(c[axis] == chips[i % 2][axis] for i, c in enumerate(chips))
        and chips[0][axis] != chips[1][axis]
        for axis in range(len(chips[0]))
    )


def layer_kernel(
    ring,
    snake,
    q_ref,
    bkv_ref,
    cache_hbm,
    prefix_ref,
    valid_ref,
    resid_ref,
    gain_ref,
    wg_hbm,
    wu_hbm,
    wd_hbm,
    out_ref,
    cache,
    wg,
    wu,
    wd,
    xg,
    acc_g,
    acc_u,
    sumsq,
    hid,
    csum,
    psend,
    precv,
    rsend,
    rrecv,
    lsend,
    lrecv,
    cache_sem,
    w_sem,
    ag_recv,
    ag_right,
    ag_left,
    ag_pair,
    p_ssem,
    p_rsem,
    r_ssem,
    r_rsem,
    l_ssem,
    l_rsem,
):
    reqs, block_len, width = q_ref.shape
    cache_len = cache.shape[1]
    head_size = cache.shape[2] // 2
    heads = width // head_size
    hidden_here = wg.shape[1]
    model_width = KVH * width
    rows = reqs * block_len
    groups = acc_g.shape[0] // rows
    pairs = KVH // CORES
    half = ring // 2
    paired = snake and ring == 2 * pairs == 8 and groups == 2
    me = lax.axis_index("ffn")
    core = me % CORES
    chip = me // CORES
    if snake:
        here = (1 - chip % 2) * (chip // 2) + (chip % 2) * (ring - 1 - chip // 2)
    else:
        here = chip

    def chip_at(offset):
        place = (here + offset + ring) % ring
        if not snake:
            return place
        back = place // half
        return (1 - back) * (2 * place) + back * (2 * (ring - 1 - place) + 1)

    partner = chip * CORES + (1 - core)
    right = chip_at(1) * CORES + core
    left = chip_at(-1) * CORES + core

    barrier = pltpu.get_barrier_semaphore()
    for other in (partner, right, left):
        pl.semaphore_signal(
            barrier, inc=1, device_id={"ffn": other}, device_id_type=pl.DeviceIdType.MESH
        )

    cache_copies = [
        pltpu.make_async_copy(cache_hbm.at[r], cache.at[r], cache_sem.at[r]) for r in range(reqs)
    ]
    for copy in cache_copies:
        copy.start()
    weight_copies = []
    for w, (source, target) in enumerate(((wg_hbm, wg), (wu_hbm, wu))):
        for h in range(KVH):
            span = pl.ds(h * width, width)
            weight_copies.append(
                pltpu.make_async_copy(source.at[span], target.at[span], w_sem.at[w, h])
            )
    down_copies = []
    for h in range(KVH):
        span = pl.ds(h * width, width)
        down_copies.append(
            pltpu.make_async_copy(wd_hbm.at[:, span], wd.at[:, span], w_sem.at[2, h])
        )
    for copy in weight_copies + down_copies:
        copy.start()

    def send(source, target, ssem, rsem, device):
        return pltpu.make_async_remote_copy(
            src_ref=source,
            dst_ref=target,
            send_sem=ssem,
            recv_sem=rsem,
            device_id={"ffn": device},
            device_id_type=pl.DeviceIdType.MESH,
        )

    def to_right(s, i):
        return send(xg.at[s, i], xg.at[s, i], ag_right.at[s, i], ag_recv.at[s, i], right)

    def to_left(s, i):
        return send(xg.at[s, i], xg.at[s, i], ag_left.at[s, i], ag_recv.at[s, i], left)

    def to_pair(s, i):
        return send(xg.at[s, i], xg.at[s, i], ag_pair.at[s, i], ag_recv.at[s, i], partner)

    def goes_right(i):
        return i < reqs // 2

    group = me // KVH
    scale = math.log2(math.e) / (head_size**0.5)
    for r in range(reqs):
        cache_copies[r].wait()
        query = q_ref[r]
        stacked = jnp.concatenate(
            [query[:, h * head_size : (h + 1) * head_size] for h in range(heads)], axis=0
        )
        contract = (((1,), (1,)), ((), ()))
        far = lax.dot_general(
            stacked, cache[r, :, :head_size], contract, preferred_element_type=jnp.float32
        )
        near = lax.dot_general(
            stacked, bkv_ref[r, :, :head_size], contract, preferred_element_type=jnp.float32
        )
        seen = prefix_ref[group * reqs + r]
        live = valid_ref[group * reqs + r]
        far_at = lax.broadcasted_iota(jnp.int32, (1, cache_len), 1)
        near_at = lax.broadcasted_iota(jnp.int32, (1, block_len), 1)
        far = jnp.where(far_at < seen, far, -1e30)
        near = jnp.where(near_at < live, near, -1e30)
        peak = jnp.maximum(
            jnp.max(far, axis=-1, keepdims=True), jnp.max(near, axis=-1, keepdims=True)
        )
        far = jnp.exp2((far - peak) * scale)
        near = jnp.exp2((near - peak) * scale)
        total = jnp.sum(far, axis=-1, keepdims=True) + jnp.sum(near, axis=-1, keepdims=True)
        inverse = 1.0 / total
        mixed = jnp.dot(
            (far * inverse).astype(jnp.bfloat16),
            cache[r, :, head_size:],
            preferred_element_type=jnp.float32,
        ) + jnp.dot(
            (near * inverse).astype(jnp.bfloat16),
            bkv_ref[r, :, head_size:],
            preferred_element_type=jnp.float32,
        )
        side = jnp.concatenate(
            [mixed[h * block_len : (h + 1) * block_len] for h in range(heads)], axis=1
        )
        xg[me, r] = (resid_ref[r].astype(jnp.float32) + side).astype(jnp.bfloat16)
        if r == 0:
            pl.semaphore_wait(barrier, 3)
        to_right(me, r).start()
        to_left(me, r).start()
        to_pair(me, r).start()

    def fold(square):
        folded = square[:, :head_size]
        for h in range(1, square.shape[1] // head_size):
            folded = folded + square[:, h * head_size : (h + 1) * head_size]
        return folded

    def absorb(s):
        mine = pl.ds(pl.multiple_of((s // KVH) * rows, rows), rows)
        span = pl.ds(pl.multiple_of((s % KVH) * width, width), width)
        block = xg[s].reshape(rows, width).astype(jnp.float32)
        sumsq[mine] += fold(block * block)
        scaled = (block * gain_ref[:, span]).astype(jnp.bfloat16)
        acc_g[mine] += jnp.dot(scaled, wg[span, :], preferred_element_type=jnp.float32)
        acc_u[mine] += jnp.dot(scaled, wu[span, :], preferred_element_type=jnp.float32)

    def absorb_heads(k, first=False):
        span = pl.ds(pl.multiple_of(k * CORES * width, CORES * width), CORES * width)
        block = jnp.concatenate(
            [
                jnp.concatenate(
                    [xg[g * KVH + k * CORES + c].reshape(rows, width) for c in range(CORES)],
                    axis=1,
                )
                for g in range(groups)
            ],
            axis=0,
        ).astype(jnp.float32)
        squares = fold(block * block)
        scaled = (block * gain_ref[:, span]).astype(jnp.bfloat16)
        gate = jnp.dot(scaled, wg[span, :], preferred_element_type=jnp.float32)
        up = jnp.dot(scaled, wu[span, :], preferred_element_type=jnp.float32)
        if first:
            sumsq[...] = squares
            acc_g[...] = gate
            acc_u[...] = up
        else:
            sumsq[...] += squares
            acc_g[...] += gate
            acc_u[...] += up

    def pair_arrived(s):
        for i in range(reqs):
            to_pair(s, i).wait_recv()

    def absorb_pair(s):
        pair_arrived(s)
        absorb(s)

    def pass_on(t, last):
        from_left = chip_at(-t) * CORES + core
        from_right = chip_at(t) * CORES + core
        for i in range(reqs):
            to_right(from_left, i).wait_recv()
            if not last or goes_right(i):
                to_right(from_left, i).start()
            to_pair(from_left, i).start()
            to_left(from_right, i).wait_recv()
            if not last or not goes_right(i):
                to_left(from_right, i).start()
            to_pair(from_right, i).start()

    def absorb_step(t):
        absorb(chip_at(-t) * CORES + core)
        absorb(chip_at(t) * CORES + core)
        absorb_pair(chip_at(-t) * CORES + 1 - core)
        absorb_pair(chip_at(t) * CORES + 1 - core)

    def from_far():
        for i in range(reqs):
            (to_right if goes_right(i) else to_left)(far_chip * CORES + core, i).wait_recv()
            to_pair(far_chip * CORES + core, i).start()

    far_chip = chip_at(half)
    other = 1 - core
    k_own = chip % pairs
    k_far = far_chip % pairs
    if paired:
        k_near = k_own + 1 - 2 * (k_own % 2)
        k_next = pairs - 1 - k_near
        pass_on(1, False)
        pair_arrived(partner)
        pass_on(2, False)
        for t in (-1, 1, -2, 2):
            pair_arrived(chip_at(t) * CORES + other)
        for copy in weight_copies:
            copy.wait()
        absorb_heads(k_own, True)
        pass_on(3, True)
        for t in (-3, 3):
            pair_arrived(chip_at(t) * CORES + other)
        absorb_heads(k_near)
        from_far()
        absorb_heads(k_next)
        pair_arrived(far_chip * CORES + other)
        absorb_heads(k_far)
    else:
        acc_g[...] = jnp.zeros_like(acc_g)
        acc_u[...] = jnp.zeros_like(acc_u)
        sumsq[...] = jnp.zeros_like(sumsq)
        pass_on(1, half == 2)
        for copy in weight_copies:
            copy.wait()
        absorb(me)
        absorb_pair(partner)
        absorb_step(1)

        def middle(t, carry):
            pass_on(t, False)
            absorb_step(t)
            return carry

        if half > 2:
            lax.fori_loop(2, half - 1, middle, 0)
            pass_on(half - 1, True)
            absorb_step(half - 1)
        from_far()
        absorb(far_chip * CORES + core)
        absorb_pair(far_chip * CORES + other)

    mean_square = jnp.sum(sumsq[...], axis=-1, keepdims=True) / model_width
    root = lax.rsqrt(mean_square + epsilon)
    gate = acc_g[...] * root
    up = acc_u[...] * root
    hid[...] = (gate * jax.nn.sigmoid(gate) * up).astype(jnp.bfloat16)

    for copy in down_copies:
        copy.wait()

    def pair_copy(k):
        return send(psend.at[k], precv.at[k], p_ssem.at[k], p_rsem.at[k], partner)

    def column_of(k, parity):
        return pl.ds(pl.multiple_of((k * CORES + parity) * width, width), width)

    def give(k):
        share = jnp.dot(hid[...], wd[:, column_of(k, other)], preferred_element_type=jnp.float32)
        psend[k] = share.astype(jnp.bfloat16).reshape(groups, reqs, block_len, width)
        pair_copy(k).start()

    def keep(k):
        share = jnp.dot(hid[...], wd[:, column_of(k, core)], preferred_element_type=jnp.float32)
        pair_copy(k).wait_recv()
        csum[k] = share.reshape(groups, reqs, block_len, width) + precv[k].astype(jnp.float32)

    def right_copy(t, i):
        return send(rsend.at[t, i], rrecv.at[t, i], r_ssem.at[t, i], r_rsem.at[t, i], right)

    def left_copy(t, i):
        return send(lsend.at[t, i], lrecv.at[t, i], l_ssem.at[t, i], l_rsem.at[t, i], left)

    sent = []

    def ring_step(t):
        for i in range(reqs):
            for copy_of, out_buf, in_buf, offset, first in (
                (right_copy, rsend, rrecv, t, goes_right(i)),
                (left_copy, lsend, lrecv, -t, not goes_right(i)),
            ):
                if t == half and not first:
                    continue
                target = chip_at(offset)
                value = csum[target % pairs, target // pairs, i]
                if t < half - 1 or (t == half - 1 and first):
                    copy_of(t, i).wait_recv()
                    value = value + in_buf[t, i].astype(jnp.float32)
                out_buf[t - 1, i] = value.astype(jnp.bfloat16)
                copy_of(t - 1, i).start()
                sent.append(copy_of(t - 1, i))

    if paired:
        give(k_far)
        give(k_near)
        keep(k_far)
        ring_step(4)
        give(k_next)
        keep(k_near)
        keep(k_next)
        ring_step(3)
        give(k_own)
        keep(k_own)
        ring_step(2)
        ring_step(1)
    else:
        for j in range(pairs):
            give(j)
        for j in range(pairs):
            keep(j)
        for t in range(half, 0, -1):
            ring_step(t)
    for i in range(reqs):
        right_copy(0, i).wait_recv()
        left_copy(0, i).wait_recv()
        value = csum[chip % pairs, chip // pairs, i]
        value = value + rrecv[0, i].astype(jnp.float32) + lrecv[0, i].astype(jnp.float32)
        out_ref[i] = (xg[me, i].astype(jnp.float32) + value).astype(jnp.bfloat16)

    for copy in sent:
        copy.wait_send()

    def pair_sent(k, carry):
        pair_copy(k).wait_send()
        return carry

    lax.fori_loop(0, pairs, pair_sent, 0)

    def gather_sent(t, carry):
        for i in range(reqs):
            to_right(chip_at(-t) * CORES + core, i).wait_send()
            to_pair(chip_at(-t) * CORES + core, i).wait_send()
            to_left(chip_at(t) * CORES + core, i).wait_send()
            to_pair(chip_at(t) * CORES + core, i).wait_send()
        return carry

    for i in range(reqs):
        to_right(me, i).wait_send()
        to_left(me, i).wait_send()
        to_pair(me, i).wait_send()
        to_pair(far_chip * CORES + core, i).wait_send()
        (to_right(chip_at(1 - half) * CORES + core, i) if goes_right(i) else to_left(
            chip_at(half - 1) * CORES + core, i
        )).wait_send()
        to_pair(chip_at(1 - half) * CORES + core, i).wait_send()
        to_pair(chip_at(half - 1) * CORES + core, i).wait_send()
    lax.fori_loop(1, half - 1, gather_sent, 0)


def body(
    snake,
    queries,
    block_kv,
    cache_kv,
    prefix_len,
    block_valid,
    resid,
    norm_gain,
    w_gate,
    w_up,
    w_down,
):
    count = lax.axis_size("ffn")
    ring = count // CORES
    half = ring // 2
    _, reqs, block_len, width = queries.shape
    hidden_here = w_gate.shape[1]
    groups = count // KVH
    rows = reqs * block_len
    pairs = KVH // CORES
    lanes = block_kv.shape[3] // 2
    bf16, f32 = jnp.bfloat16, jnp.float32
    vmem = pl.BlockSpec(memory_space=pltpu.VMEM)
    smem = pl.BlockSpec(memory_space=pltpu.SMEM)
    hbm = pl.BlockSpec(memory_space=pl.ANY)
    dma = pltpu.SemaphoreType.DMA
    flops = 2 * groups * rows * KVH * width * hidden_here * 3
    out = pl.pallas_call(
        functools.partial(layer_kernel, ring, snake),
        out_shape=jax.ShapeDtypeStruct((reqs, block_len, width), bf16),
        in_specs=[vmem, vmem, hbm, smem, smem, vmem, vmem, hbm, hbm, hbm],
        out_specs=vmem,
        scratch_shapes=[
            pltpu.VMEM(cache_kv.shape[1:], bf16),
            pltpu.VMEM(w_gate.shape, bf16),
            pltpu.VMEM(w_up.shape, bf16),
            pltpu.VMEM(w_down.shape, bf16),
            pltpu.VMEM((count, reqs, block_len, width), bf16),
            pltpu.VMEM((groups * rows, hidden_here), f32),
            pltpu.VMEM((groups * rows, hidden_here), f32),
            pltpu.VMEM((groups * rows, lanes), f32),
            pltpu.VMEM((groups * rows, hidden_here), bf16),
            pltpu.VMEM((pairs, groups, reqs, block_len, width), f32),
            pltpu.VMEM((pairs, groups, reqs, block_len, width), bf16),
            pltpu.VMEM((pairs, groups, reqs, block_len, width), bf16),
            pltpu.VMEM((half, reqs, block_len, width), bf16),
            pltpu.VMEM((half, reqs, block_len, width), bf16),
            pltpu.VMEM((half, reqs, block_len, width), bf16),
            pltpu.VMEM((half, reqs, block_len, width), bf16),
            dma((reqs,)),
            dma((3, KVH)),
            dma((count, reqs)),
            dma((count, reqs)),
            dma((count, reqs)),
            dma((count, reqs)),
            dma((pairs,)),
            dma((pairs,)),
            dma((half, reqs)),
            dma((half, reqs)),
            dma((half, reqs)),
            dma((half, reqs)),
        ],
        compiler_params=pltpu.CompilerParams(
            collective_id=0, has_side_effects=True, vmem_limit_bytes=57 * 1024 * 1024
        ),
        cost_estimate=pl.CostEstimate(
            flops=flops, bytes_accessed=6 * KVH * width * hidden_here, transcendentals=0
        ),
    )(
        queries[0],
        block_kv[0],
        cache_kv[0],
        prefix_len,
        block_valid,
        resid[0],
        norm_gain.reshape(1, -1),
        w_gate,
        w_up,
        w_down,
    )
    return out[None]


def solution(mesh):
    in_specs = (
        P(("groups", "ffn"), None, None, None),
        P(("groups", "ffn"), None, None, None),
        P(("groups", "ffn"), None, None, None),
        P("groups"),
        P("groups"),
        P(("groups", "ffn"), None, None, None),
        P(),
        P(None, "ffn"),
        P(None, "ffn"),
        P("ffn", None),
    )
    out_specs = P(("groups", "ffn"), None, None, None)
    return jax.shard_map(
        functools.partial(body, ring_is_snake(mesh)),
        mesh=mesh,
        in_specs=in_specs,
        out_specs=out_specs,
        check_vma=False,
    )
```

```python
import functools
import math

import jax
import jax.numpy as jnp
from jax import lax
from jax.experimental import pallas as pl
from jax.experimental.pallas import tpu as pltpu
from jax.sharding import PartitionSpec as P

KVH = 8
CORES = 2

epsilon = 1e-05


def ring_is_snake(mesh):
    row = mesh.devices.reshape(mesh.shape["groups"], mesh.shape["ffn"])[0]
    chips = [getattr(row[i], "coords", None) for i in range(0, len(row), CORES)]
    if len(chips) < 4 or any(c is None for c in chips):
        return False
    return any(
        all(c[axis] == chips[i % 2][axis] for i, c in enumerate(chips))
        and chips[0][axis] != chips[1][axis]
        for axis in range(len(chips[0]))
    )


def layer_kernel(
    ring,
    snake,
    q_ref,
    bkv_ref,
    cache_hbm,
    prefix_ref,
    valid_ref,
    resid_ref,
    gain_ref,
    wg_hbm,
    wu_hbm,
    wd_hbm,
    out_ref,
    cache,
    wg,
    wu,
    wd,
    xg,
    acc_g,
    acc_u,
    sumsq,
    hid,
    csum,
    psend,
    precv,
    rsend,
    rrecv,
    lsend,
    lrecv,
    cache_sem,
    w_sem,
    ag_recv,
    ag_right,
    ag_left,
    ag_pair,
    p_ssem,
    p_rsem,
    r_ssem,
    r_rsem,
    l_ssem,
    l_rsem,
):
    reqs, block_len, width = q_ref.shape
    cache_len = cache.shape[1]
    head_size = cache.shape[2] // 2
    heads = width // head_size
    hidden_here = wg.shape[1]
    model_width = KVH * width
    rows = reqs * block_len
    groups = acc_g.shape[0] // rows
    pairs = KVH // CORES
    half = ring // 2
    paired = snake and ring == 2 * pairs == 8 and groups == 2
    me = lax.axis_index("ffn")
    core = me % CORES
    chip = me // CORES
    if snake:
        here = (1 - chip % 2) * (chip // 2) + (chip % 2) * (ring - 1 - chip // 2)
    else:
        here = chip

    def chip_at(offset):
        place = (here + offset + ring) % ring
        if not snake:
            return place
        back = place // half
        return (1 - back) * (2 * place) + back * (2 * (ring - 1 - place) + 1)

    partner = chip * CORES + (1 - core)
    right = chip_at(1) * CORES + core
    left = chip_at(-1) * CORES + core

    barrier = pltpu.get_barrier_semaphore()
    for other in (partner, right, left):
        pl.semaphore_signal(
            barrier, inc=1, device_id={"ffn": other}, device_id_type=pl.DeviceIdType.MESH
        )

    def cache_copy(r):
        return pltpu.make_async_copy(cache_hbm.at[r], cache.at[r], cache_sem.at[r])

    for r in range(reqs):
        cache_copy(r).start()
    weight_copies = []
    for w, (source, target) in enumerate(((wg_hbm, wg), (wu_hbm, wu))):
        for h in range(KVH):
            span = pl.ds(h * width, width)
            weight_copies.append(
                pltpu.make_async_copy(source.at[span], target.at[span], w_sem.at[w, h])
            )
    down_copies = []
    for h in range(KVH):
        span = pl.ds(h * width, width)
        down_copies.append(
            pltpu.make_async_copy(wd_hbm.at[:, span], wd.at[:, span], w_sem.at[2, h])
        )
    for copy in weight_copies + down_copies:
        copy.start()

    def send(source, target, ssem, rsem, device):
        return pltpu.make_async_remote_copy(
            src_ref=source,
            dst_ref=target,
            send_sem=ssem,
            recv_sem=rsem,
            device_id={"ffn": device},
            device_id_type=pl.DeviceIdType.MESH,
        )

    def to_right(s, i):
        return send(xg.at[s, i], xg.at[s, i], ag_right.at[s, i], ag_recv.at[s, i], right)

    def to_left(s, i):
        return send(xg.at[s, i], xg.at[s, i], ag_left.at[s, i], ag_recv.at[s, i], left)

    def to_pair(s, i):
        return send(xg.at[s, i], xg.at[s, i], ag_pair.at[s, i], ag_recv.at[s, i], partner)

    def goes_right(i):
        return i < reqs // 2

    group = me // KVH
    scale = math.log2(math.e) / (head_size**0.5)
    parts = 2 if heads % 2 == 0 else 1
    part_heads = heads // parts
    part_width = part_heads * head_size

    def attend(step, carry):
        r = step // parts
        part = step % parts

        @pl.when(part == 0)
        def _():
            cache_copy(r).wait()

        columns = pl.ds(pl.multiple_of(part * part_width, part_width), part_width)
        query = q_ref[r, :, columns]
        stacked = jnp.concatenate(
            [query[:, h * head_size : (h + 1) * head_size] for h in range(part_heads)], axis=0
        )
        contract = (((1,), (1,)), ((), ()))
        far = lax.dot_general(
            stacked, cache[r, :, :head_size], contract, preferred_element_type=jnp.float32
        )
        near = lax.dot_general(
            stacked, bkv_ref[r, :, :head_size], contract, preferred_element_type=jnp.float32
        )
        seen = prefix_ref[group * reqs + r]
        live = valid_ref[group * reqs + r]
        far_at = lax.broadcasted_iota(jnp.int32, (1, cache_len), 1)
        near_at = lax.broadcasted_iota(jnp.int32, (1, block_len), 1)
        far = jnp.where(far_at < seen, far, -1e30)
        near = jnp.where(near_at < live, near, -1e30)
        peak = jnp.maximum(
            jnp.max(far, axis=-1, keepdims=True), jnp.max(near, axis=-1, keepdims=True)
        )
        far = jnp.exp2((far - peak) * scale)
        near = jnp.exp2((near - peak) * scale)
        total = jnp.sum(far, axis=-1, keepdims=True) + jnp.sum(near, axis=-1, keepdims=True)
        inverse = 1.0 / total
        mixed = jnp.dot(
            (far * inverse).astype(jnp.bfloat16),
            cache[r, :, head_size:],
            preferred_element_type=jnp.float32,
        ) + jnp.dot(
            (near * inverse).astype(jnp.bfloat16),
            bkv_ref[r, :, head_size:],
            preferred_element_type=jnp.float32,
        )
        side = jnp.concatenate(
            [mixed[h * block_len : (h + 1) * block_len] for h in range(part_heads)], axis=1
        )
        state = resid_ref[r, :, columns].astype(jnp.float32) + side
        xg[me, r, :, columns] = state.astype(jnp.bfloat16)

        @pl.when(step == parts - 1)
        def _():
            pl.semaphore_wait(barrier, 3)

        @pl.when(part == parts - 1)
        def _():
            to_right(me, r).start()
            to_left(me, r).start()
            to_pair(me, r).start()

        return carry

    lax.fori_loop(0, reqs * parts, attend, 0)

    def fold(square):
        folded = square[:, :head_size]
        for h in range(1, square.shape[1] // head_size):
            folded = folded + square[:, h * head_size : (h + 1) * head_size]
        return folded

    def absorb(s):
        mine = pl.ds(pl.multiple_of((s // KVH) * rows, rows), rows)
        span = pl.ds(pl.multiple_of((s % KVH) * width, width), width)
        block = xg[s].reshape(rows, width).astype(jnp.float32)
        sumsq[mine] += fold(block * block)
        scaled = (block * gain_ref[:, span]).astype(jnp.bfloat16)
        acc_g[mine] += jnp.dot(scaled, wg[span, :], preferred_element_type=jnp.float32)
        acc_u[mine] += jnp.dot(scaled, wu[span, :], preferred_element_type=jnp.float32)

    def absorb_head(h):
        span = pl.ds(pl.multiple_of(h * width, width), width)
        block = jnp.concatenate(
            [xg[g * KVH + h].reshape(rows, width) for g in range(groups)], axis=0
        ).astype(jnp.float32)
        sumsq[...] += fold(block * block)
        scaled = (block * gain_ref[:, span]).astype(jnp.bfloat16)
        acc_g[...] += jnp.dot(scaled, wg[span, :], preferred_element_type=jnp.float32)
        acc_u[...] += jnp.dot(scaled, wu[span, :], preferred_element_type=jnp.float32)

    def pair_arrived(s):
        for i in range(reqs):
            to_pair(s, i).wait_recv()

    def absorb_pair(s):
        pair_arrived(s)
        absorb(s)

    def pass_on(t, last):
        from_left = chip_at(-t) * CORES + core
        from_right = chip_at(t) * CORES + core
        for i in range(reqs):
            to_right(from_left, i).wait_recv()
            if not last or goes_right(i):
                to_right(from_left, i).start()
            to_pair(from_left, i).start()
            to_left(from_right, i).wait_recv()
            if not last or not goes_right(i):
                to_left(from_right, i).start()
            to_pair(from_right, i).start()

    def absorb_step(t):
        absorb(chip_at(-t) * CORES + core)
        absorb(chip_at(t) * CORES + core)
        absorb_pair(chip_at(-t) * CORES + 1 - core)
        absorb_pair(chip_at(t) * CORES + 1 - core)

    def from_far():
        for i in range(reqs):
            (to_right if goes_right(i) else to_left)(far_chip * CORES + core, i).wait_recv()
            to_pair(far_chip * CORES + core, i).start()

    far_chip = chip_at(half)
    other = 1 - core
    acc_g[...] = jnp.zeros_like(acc_g)
    acc_u[...] = jnp.zeros_like(acc_u)
    sumsq[...] = jnp.zeros_like(sumsq)

    def flipped(bits):
        low = (chip + bits) % 2
        high = (chip // 2 + bits // 2) % 2
        return 2 * high + low

    if paired:
        def from_both(t):
            pair_arrived(chip_at(-t) * CORES + other)
            pair_arrived(chip_at(t) * CORES + other)

        def stage(step, carry):
            j = step // CORES

            @pl.when(step == 0)
            def _():
                pass_on(1, False)
                pair_arrived(partner)
                pass_on(2, False)
                from_both(1)
                from_both(2)
                for copy in weight_copies:
                    copy.wait()

            @pl.when(step == CORES)
            def _():
                pass_on(3, True)
                from_both(3)

            @pl.when(step == 2 * CORES)
            def _():
                from_far()

            @pl.when(step == 3 * CORES)
            def _():
                pair_arrived(far_chip * CORES + other)

            absorb_head(flipped(j) * CORES + step % CORES)
            return carry

        lax.fori_loop(0, KVH, stage, 0)
    else:
        pass_on(1, half == 2)
        for copy in weight_copies:
            copy.wait()
        absorb(me)
        absorb_pair(partner)
        absorb_step(1)

        def middle(t, carry):
            pass_on(t, False)
            absorb_step(t)
            return carry

        if half > 2:
            lax.fori_loop(2, half - 1, middle, 0)
            pass_on(half - 1, True)
            absorb_step(half - 1)
        from_far()
        absorb(far_chip * CORES + core)
        absorb_pair(far_chip * CORES + other)

    mean_square = jnp.sum(sumsq[...], axis=-1, keepdims=True) / model_width
    root = lax.rsqrt(mean_square + epsilon)
    gate = acc_g[...] * root
    up = acc_u[...] * root
    hid[...] = (gate * jax.nn.sigmoid(gate) * up).astype(jnp.bfloat16)

    for copy in down_copies:
        copy.wait()

    def pair_copy(k):
        return send(psend.at[k], precv.at[k], p_ssem.at[k], p_rsem.at[k], partner)

    def column_of(k, parity):
        return pl.ds(pl.multiple_of((k * CORES + parity) * width, width), width)

    def give(k):
        share = jnp.dot(hid[...], wd[:, column_of(k, other)], preferred_element_type=jnp.float32)
        psend[k] = share.astype(jnp.bfloat16).reshape(groups, reqs, block_len, width)
        pair_copy(k).start()

    def keep(k):
        share = jnp.dot(hid[...], wd[:, column_of(k, core)], preferred_element_type=jnp.float32)
        pair_copy(k).wait_recv()
        csum[k] = share.reshape(groups, reqs, block_len, width) + precv[k].astype(jnp.float32)

    def right_copy(t, i):
        return send(rsend.at[t, i], rrecv.at[t, i], r_ssem.at[t, i], r_rsem.at[t, i], right)

    def left_copy(t, i):
        return send(lsend.at[t, i], lrecv.at[t, i], l_ssem.at[t, i], l_rsem.at[t, i], left)

    def ring_move(t, i, first, copy_of, out_buf, in_buf, offset):
        target = chip_at(offset)

        def own():
            return csum[target % pairs, target // pairs, i]

        fed = (t < half - 1) | ((t == half - 1) & first)

        @pl.when(fed)
        def _():
            copy_of(t, i).wait_recv()
            total = own() + in_buf[t, i].astype(jnp.float32)
            out_buf[t - 1, i] = total.astype(jnp.bfloat16)

        @pl.when(jnp.logical_not(fed))
        def _():
            out_buf[t - 1, i] = own().astype(jnp.bfloat16)

        copy_of(t - 1, i).start()

    def ring_step(t):
        def piece(i, carry):
            first = i < reqs // 2

            @pl.when((t < half) | first)
            def _():
                ring_move(t, i, first, right_copy, rsend, rrecv, t)

            @pl.when((t < half) | jnp.logical_not(first))
            def _():
                ring_move(t, i, jnp.logical_not(first), left_copy, lsend, lrecv, -t)

            return carry

        lax.fori_loop(0, reqs, piece, 0)

    if paired:
        def down(j, carry):
            @pl.when(j < pairs)
            def _():
                give(flipped(pairs - 1 - j))

            @pl.when((j > 0) & (j <= pairs))
            def _():
                keep(flipped(pairs - j))

            @pl.when((j == 1) | (j > 2))
            def _():
                ring_step(jnp.minimum(half, half + 2 - j))

            return carry

        lax.fori_loop(0, pairs + 2, down, 0)
    else:

        def give_one(j, carry):
            give(j)
            return carry

        def keep_one(j, carry):
            keep(j)
            return carry

        def ring_one(j, carry):
            ring_step(half - j)
            return carry

        lax.fori_loop(0, pairs, give_one, 0)
        lax.fori_loop(0, pairs, keep_one, 0)
        lax.fori_loop(0, half, ring_one, 0)
    for i in range(reqs):
        right_copy(0, i).wait_recv()
        left_copy(0, i).wait_recv()
        value = csum[chip % pairs, chip // pairs, i]
        value = value + rrecv[0, i].astype(jnp.float32) + lrecv[0, i].astype(jnp.float32)
        out_ref[i] = (xg[me, i].astype(jnp.float32) + value).astype(jnp.bfloat16)

    def ring_sent(t, carry):
        for i in range(reqs):
            right_copy(t, i).wait_send()
            left_copy(t, i).wait_send()
        return carry

    lax.fori_loop(0, half - 1, ring_sent, 0)
    for i in range(reqs):
        (right_copy if goes_right(i) else left_copy)(half - 1, i).wait_send()

    def pair_sent(k, carry):
        pair_copy(k).wait_send()
        return carry

    lax.fori_loop(0, pairs, pair_sent, 0)

    def gather_sent(t, carry):
        for i in range(reqs):
            to_right(chip_at(-t) * CORES + core, i).wait_send()
            to_pair(chip_at(-t) * CORES + core, i).wait_send()
            to_left(chip_at(t) * CORES + core, i).wait_send()
            to_pair(chip_at(t) * CORES + core, i).wait_send()
        return carry

    for i in range(reqs):
        to_right(me, i).wait_send()
        to_left(me, i).wait_send()
        to_pair(me, i).wait_send()
        to_pair(far_chip * CORES + core, i).wait_send()
        (to_right(chip_at(1 - half) * CORES + core, i) if goes_right(i) else to_left(
            chip_at(half - 1) * CORES + core, i
        )).wait_send()
        to_pair(chip_at(1 - half) * CORES + core, i).wait_send()
        to_pair(chip_at(half - 1) * CORES + core, i).wait_send()
    lax.fori_loop(1, half - 1, gather_sent, 0)


def body(
    snake,
    queries,
    block_kv,
    cache_kv,
    prefix_len,
    block_valid,
    resid,
    norm_gain,
    w_gate,
    w_up,
    w_down,
):
    count = lax.axis_size("ffn")
    ring = count // CORES
    half = ring // 2
    _, reqs, block_len, width = queries.shape
    hidden_here = w_gate.shape[1]
    groups = count // KVH
    rows = reqs * block_len
    pairs = KVH // CORES
    lanes = block_kv.shape[3] // 2
    bf16, f32 = jnp.bfloat16, jnp.float32
    vmem = pl.BlockSpec(memory_space=pltpu.VMEM)
    smem = pl.BlockSpec(memory_space=pltpu.SMEM)
    hbm = pl.BlockSpec(memory_space=pl.ANY)
    dma = pltpu.SemaphoreType.DMA
    flops = 2 * groups * rows * KVH * width * hidden_here * 3
    out = pl.pallas_call(
        functools.partial(layer_kernel, ring, snake),
        out_shape=jax.ShapeDtypeStruct((reqs, block_len, width), bf16),
        in_specs=[vmem, vmem, hbm, smem, smem, vmem, vmem, hbm, hbm, hbm],
        out_specs=vmem,
        scratch_shapes=[
            pltpu.VMEM(cache_kv.shape[1:], bf16),
            pltpu.VMEM(w_gate.shape, bf16),
            pltpu.VMEM(w_up.shape, bf16),
            pltpu.VMEM(w_down.shape, bf16),
            pltpu.VMEM((count, reqs, block_len, width), bf16),
            pltpu.VMEM((groups * rows, hidden_here), f32),
            pltpu.VMEM((groups * rows, hidden_here), f32),
            pltpu.VMEM((groups * rows, lanes), f32),
            pltpu.VMEM((groups * rows, hidden_here), bf16),
            pltpu.VMEM((pairs, groups, reqs, block_len, width), f32),
            pltpu.VMEM((pairs, groups, reqs, block_len, width), bf16),
            pltpu.VMEM((pairs, groups, reqs, block_len, width), bf16),
            pltpu.VMEM((half, reqs, block_len, width), bf16),
            pltpu.VMEM((half, reqs, block_len, width), bf16),
            pltpu.VMEM((half, reqs, block_len, width), bf16),
            pltpu.VMEM((half, reqs, block_len, width), bf16),
            dma((reqs,)),
            dma((3, KVH)),
            dma((count, reqs)),
            dma((count, reqs)),
            dma((count, reqs)),
            dma((count, reqs)),
            dma((pairs,)),
            dma((pairs,)),
            dma((half, reqs)),
            dma((half, reqs)),
            dma((half, reqs)),
            dma((half, reqs)),
        ],
        compiler_params=pltpu.CompilerParams(
            collective_id=0, has_side_effects=True, vmem_limit_bytes=57 * 1024 * 1024
        ),
        cost_estimate=pl.CostEstimate(
            flops=flops, bytes_accessed=6 * KVH * width * hidden_here, transcendentals=0
        ),
    )(
        queries[0],
        block_kv[0],
        cache_kv[0],
        prefix_len,
        block_valid,
        resid[0],
        norm_gain.reshape(1, -1),
        w_gate,
        w_up,
        w_down,
    )
    return out[None]


def solution(mesh):
    in_specs = (
        P(("groups", "ffn"), None, None, None),
        P(("groups", "ffn"), None, None, None),
        P(("groups", "ffn"), None, None, None),
        P("groups"),
        P("groups"),
        P(("groups", "ffn"), None, None, None),
        P(),
        P(None, "ffn"),
        P(None, "ffn"),
        P("ffn", None),
    )
    out_specs = P(("groups", "ffn"), None, None, None)
    return jax.shard_map(
        functools.partial(body, ring_is_snake(mesh)),
        mesh=mesh,
        in_specs=in_specs,
        out_specs=out_specs,
        check_vma=False,
    )
```

```python
import functools
import math

import jax
import jax.numpy as jnp
from jax import lax
from jax.experimental import pallas as pl
from jax.experimental.pallas import tpu as pltpu
from jax.sharding import PartitionSpec as P

KVH = 8
CORES = 2

epsilon = 1e-05


def ring_is_snake(mesh):
    row = mesh.devices.reshape(mesh.shape["groups"], mesh.shape["ffn"])[0]
    chips = [getattr(row[i], "coords", None) for i in range(0, len(row), CORES)]
    if len(chips) < 4 or any(c is None for c in chips):
        return False
    return any(
        all(c[axis] == chips[i % 2][axis] for i, c in enumerate(chips))
        and chips[0][axis] != chips[1][axis]
        for axis in range(len(chips[0]))
    )


def layer_kernel(
    ring,
    snake,
    q_ref,
    bkv_ref,
    cache_hbm,
    prefix_ref,
    valid_ref,
    resid_ref,
    gain_ref,
    wg_hbm,
    wu_hbm,
    wd_hbm,
    out_ref,
    cache,
    wg,
    wu,
    wd,
    xg,
    acc_g,
    acc_u,
    sumsq,
    hid,
    csum,
    psend,
    precv,
    rsend,
    rrecv,
    lsend,
    lrecv,
    cache_sem,
    w_sem,
    ag_recv,
    ag_right,
    ag_left,
    ag_pair,
    p_ssem,
    p_rsem,
    r_ssem,
    r_rsem,
    l_ssem,
    l_rsem,
):
    reqs, block_len, width = q_ref.shape
    cache_len = cache.shape[1]
    head_size = cache.shape[2] // 2
    heads = width // head_size
    hidden_here = wg.shape[1]
    model_width = KVH * width
    rows = reqs * block_len
    groups = acc_g.shape[0] // rows
    pairs = KVH // CORES
    half = ring // 2
    paired = snake and ring == 2 * pairs == 8 and groups == 2
    me = lax.axis_index("ffn")
    core = me % CORES
    chip = me // CORES
    if snake:
        here = (1 - chip % 2) * (chip // 2) + (chip % 2) * (ring - 1 - chip // 2)
    else:
        here = chip

    def chip_at(offset):
        place = (here + offset + ring) % ring
        if not snake:
            return place
        back = place // half
        return (1 - back) * (2 * place) + back * (2 * (ring - 1 - place) + 1)

    partner = chip * CORES + (1 - core)
    right = chip_at(1) * CORES + core
    left = chip_at(-1) * CORES + core

    barrier = pltpu.get_barrier_semaphore()
    for other in (partner, right, left):
        pl.semaphore_signal(
            barrier, inc=1, device_id={"ffn": other}, device_id_type=pl.DeviceIdType.MESH
        )

    def cache_copy(r):
        return pltpu.make_async_copy(cache_hbm.at[r], cache.at[r], cache_sem.at[r])

    for r in range(reqs):
        cache_copy(r).start()

    def flipped(bits):
        low = (chip + bits) % 2
        high = (chip // 2 + bits // 2) % 2
        return 2 * high + low

    far_chip = chip_at(half)
    other = 1 - core

    def gate_copy(h):
        span = pl.ds(pl.multiple_of(h * width, width), width)
        return pltpu.make_async_copy(wg_hbm.at[span], wg.at[span], w_sem.at[0, h])

    def up_copy(h):
        span = pl.ds(pl.multiple_of(h * width, width), width)
        return pltpu.make_async_copy(wu_hbm.at[span], wu.at[span], w_sem.at[1, h])

    def down_copy(h):
        span = pl.ds(pl.multiple_of(h * width, width), width)
        return pltpu.make_async_copy(wd_hbm.at[:, span], wd.at[:, span], w_sem.at[2, h])

    def head_at(step):
        return flipped(step // CORES) * CORES + step % CORES if paired else step

    def start_gate_up(step, carry):
        gate_copy(head_at(step)).start()
        up_copy(head_at(step)).start()
        return carry

    def wait_gate_up(step, carry):
        gate_copy(head_at(step)).wait()
        up_copy(head_at(step)).wait()
        return carry

    def start_down(j, carry):
        @pl.when(j < pairs)
        def _():
            down_copy(give_chip(j) * CORES + other).start()

        @pl.when(j > 0)
        def _():
            down_copy(give_chip(j - 1) * CORES + core).start()

        return carry

    def give_chip(j):
        return flipped(pairs - 1 - j) if paired else j

    def send(source, target, ssem, rsem, device):
        return pltpu.make_async_remote_copy(
            src_ref=source,
            dst_ref=target,
            send_sem=ssem,
            recv_sem=rsem,
            device_id={"ffn": device},
            device_id_type=pl.DeviceIdType.MESH,
        )

    def to_right(s, i):
        return send(xg.at[s, i], xg.at[s, i], ag_right.at[s, i], ag_recv.at[s, i], right)

    def to_left(s, i):
        return send(xg.at[s, i], xg.at[s, i], ag_left.at[s, i], ag_recv.at[s, i], left)

    def to_pair(s, i):
        return send(xg.at[s, i], xg.at[s, i], ag_pair.at[s, i], ag_recv.at[s, i], partner)

    def goes_right(i):
        return i < reqs // 2

    group = me // KVH
    scale = math.log2(math.e) / (head_size**0.5)
    parts = 2 if heads % 2 == 0 else 1
    part_heads = heads // parts
    part_width = part_heads * head_size

    def attend(step, carry):
        r = step // parts
        part = step % parts

        @pl.when(step == 0)
        def _():
            for i in range(reqs):
                cache_copy(i).wait()
            lax.fori_loop(0, KVH, start_gate_up, 0)

        columns = pl.ds(pl.multiple_of(part * part_width, part_width), part_width)
        query = q_ref[r, :, columns]
        stacked = jnp.concatenate(
            [query[:, h * head_size : (h + 1) * head_size] for h in range(part_heads)], axis=0
        )
        contract = (((1,), (1,)), ((), ()))
        far = lax.dot_general(
            stacked, cache[r, :, :head_size], contract, preferred_element_type=jnp.float32
        )
        near = lax.dot_general(
            stacked, bkv_ref[r, :, :head_size], contract, preferred_element_type=jnp.float32
        )
        seen = prefix_ref[group * reqs + r]
        live = valid_ref[group * reqs + r]
        far_at = lax.broadcasted_iota(jnp.int32, (1, cache_len), 1)
        near_at = lax.broadcasted_iota(jnp.int32, (1, block_len), 1)
        far = jnp.where(far_at < seen, far, -1e30)
        near = jnp.where(near_at < live, near, -1e30)
        peak = jnp.maximum(
            jnp.max(far, axis=-1, keepdims=True), jnp.max(near, axis=-1, keepdims=True)
        )
        far = jnp.exp2((far - peak) * scale)
        near = jnp.exp2((near - peak) * scale)
        total = jnp.sum(far, axis=-1, keepdims=True) + jnp.sum(near, axis=-1, keepdims=True)
        inverse = 1.0 / total
        mixed = jnp.dot(
            (far * inverse).astype(jnp.bfloat16),
            cache[r, :, head_size:],
            preferred_element_type=jnp.float32,
        ) + jnp.dot(
            (near * inverse).astype(jnp.bfloat16),
            bkv_ref[r, :, head_size:],
            preferred_element_type=jnp.float32,
        )
        side = jnp.concatenate(
            [mixed[h * block_len : (h + 1) * block_len] for h in range(part_heads)], axis=1
        )
        state = resid_ref[r, :, columns].astype(jnp.float32) + side
        xg[me, r, :, columns] = state.astype(jnp.bfloat16)

        @pl.when(step == parts - 1)
        def _():
            pl.semaphore_wait(barrier, 3)

        @pl.when(part == parts - 1)
        def _():
            to_right(me, r).start()
            to_left(me, r).start()
            to_pair(me, r).start()

        return carry

    lax.fori_loop(0, reqs * parts, attend, 0)

    def fold(square):
        folded = square[:, :head_size]
        for h in range(1, square.shape[1] // head_size):
            folded = folded + square[:, h * head_size : (h + 1) * head_size]
        return folded

    def absorb(s):
        mine = pl.ds(pl.multiple_of((s // KVH) * rows, rows), rows)
        span = pl.ds(pl.multiple_of((s % KVH) * width, width), width)
        block = xg[s].reshape(rows, width).astype(jnp.float32)
        sumsq[mine] += fold(block * block)
        scaled = (block * gain_ref[:, span]).astype(jnp.bfloat16)
        acc_g[mine] += jnp.dot(scaled, wg[span, :], preferred_element_type=jnp.float32)
        acc_u[mine] += jnp.dot(scaled, wu[span, :], preferred_element_type=jnp.float32)

    def absorb_head(h):
        span = pl.ds(pl.multiple_of(h * width, width), width)
        block = jnp.concatenate(
            [xg[g * KVH + h].reshape(rows, width) for g in range(groups)], axis=0
        ).astype(jnp.float32)
        sumsq[...] += fold(block * block)
        scaled = (block * gain_ref[:, span]).astype(jnp.bfloat16)
        acc_g[...] += jnp.dot(scaled, wg[span, :], preferred_element_type=jnp.float32)
        acc_u[...] += jnp.dot(scaled, wu[span, :], preferred_element_type=jnp.float32)

    def pair_arrived(s):
        for i in range(reqs):
            to_pair(s, i).wait_recv()

    def absorb_pair(s):
        pair_arrived(s)
        absorb(s)

    def pass_on(t, last):
        from_left = chip_at(-t) * CORES + core
        from_right = chip_at(t) * CORES + core
        for i in range(reqs):
            to_right(from_left, i).wait_recv()
            if not last or goes_right(i):
                to_right(from_left, i).start()
            to_pair(from_left, i).start()
            to_left(from_right, i).wait_recv()
            if not last or not goes_right(i):
                to_left(from_right, i).start()
            to_pair(from_right, i).start()

    def absorb_step(t):
        absorb(chip_at(-t) * CORES + core)
        absorb(chip_at(t) * CORES + core)
        absorb_pair(chip_at(-t) * CORES + 1 - core)
        absorb_pair(chip_at(t) * CORES + 1 - core)

    def from_far():
        for i in range(reqs):
            (to_right if goes_right(i) else to_left)(far_chip * CORES + core, i).wait_recv()
            to_pair(far_chip * CORES + core, i).start()

    acc_g[...] = jnp.zeros_like(acc_g)
    acc_u[...] = jnp.zeros_like(acc_u)
    sumsq[...] = jnp.zeros_like(sumsq)

    if paired:
        def from_both(t):
            pair_arrived(chip_at(-t) * CORES + other)
            pair_arrived(chip_at(t) * CORES + other)

        pass_on(1, False)
        pair_arrived(partner)
        pass_on(2, False)
        lax.fori_loop(0, pairs + 1, start_down, 0)
        from_both(1)
        from_both(2)
        pass_on(3, True)

        def stage(step, carry):
            @pl.when(step == CORES)
            def _():
                from_both(3)
                from_far()

            @pl.when(step == 3 * CORES)
            def _():
                pair_arrived(far_chip * CORES + other)

            wait_gate_up(step, 0)
            absorb_head(head_at(step))
            return carry

        lax.fori_loop(0, KVH, stage, 0)
    else:
        pass_on(1, half == 2)
        lax.fori_loop(0, pairs + 1, start_down, 0)
        lax.fori_loop(0, KVH, wait_gate_up, 0)
        absorb(me)
        absorb_pair(partner)
        absorb_step(1)

        def middle(t, carry):
            pass_on(t, False)
            absorb_step(t)
            return carry

        if half > 2:
            lax.fori_loop(2, half - 1, middle, 0)
            pass_on(half - 1, True)
            absorb_step(half - 1)
        from_far()
        absorb(far_chip * CORES + core)
        absorb_pair(far_chip * CORES + other)

    mean_square = jnp.sum(sumsq[...], axis=-1, keepdims=True) / model_width
    root = lax.rsqrt(mean_square + epsilon)
    gate = acc_g[...] * root
    up = acc_u[...] * root
    hid[...] = (gate * jax.nn.sigmoid(gate) * up).astype(jnp.bfloat16)

    def pair_copy(k):
        return send(psend.at[k], precv.at[k], p_ssem.at[k], p_rsem.at[k], partner)

    def column_of(k, parity):
        return pl.ds(pl.multiple_of((k * CORES + parity) * width, width), width)

    def give(k):
        down_copy(k * CORES + other).wait()
        share = jnp.dot(hid[...], wd[:, column_of(k, other)], preferred_element_type=jnp.float32)
        psend[k] = share.astype(jnp.bfloat16).reshape(groups, reqs, block_len, width)
        pair_copy(k).start()

    def keep(k):
        down_copy(k * CORES + core).wait()
        share = jnp.dot(hid[...], wd[:, column_of(k, core)], preferred_element_type=jnp.float32)
        pair_copy(k).wait_recv()
        csum[k] = share.reshape(groups, reqs, block_len, width) + precv[k].astype(jnp.float32)

    def right_copy(t, i):
        return send(rsend.at[t, i], rrecv.at[t, i], r_ssem.at[t, i], r_rsem.at[t, i], right)

    def left_copy(t, i):
        return send(lsend.at[t, i], lrecv.at[t, i], l_ssem.at[t, i], l_rsem.at[t, i], left)

    def ring_move(t, i, first, copy_of, out_buf, in_buf, offset):
        target = chip_at(offset)

        def own():
            return csum[target % pairs, target // pairs, i]

        fed = (t < half - 1) | ((t == half - 1) & first)

        @pl.when(fed)
        def _():
            copy_of(t, i).wait_recv()
            total = own() + in_buf[t, i].astype(jnp.float32)
            out_buf[t - 1, i] = total.astype(jnp.bfloat16)

        @pl.when(jnp.logical_not(fed))
        def _():
            out_buf[t - 1, i] = own().astype(jnp.bfloat16)

        copy_of(t - 1, i).start()

    def ring_step(t):
        def piece(i, carry):
            first = i < reqs // 2

            @pl.when((t < half) | first)
            def _():
                ring_move(t, i, first, right_copy, rsend, rrecv, t)

            @pl.when((t < half) | jnp.logical_not(first))
            def _():
                ring_move(t, i, jnp.logical_not(first), left_copy, lsend, lrecv, -t)

            return carry

        lax.fori_loop(0, reqs, piece, 0)

    if paired:
        def down(j, carry):
            @pl.when(j < pairs)
            def _():
                give(give_chip(j))

            @pl.when((j > 0) & (j <= pairs))
            def _():
                keep(give_chip(j - 1))

            @pl.when((j == 1) | (j > 2))
            def _():
                ring_step(jnp.minimum(half, half + 2 - j))

            return carry

        lax.fori_loop(0, pairs + 2, down, 0)
    else:

        def give_one(j, carry):
            give(j)
            return carry

        def keep_one(j, carry):
            keep(j)
            return carry

        def ring_one(j, carry):
            ring_step(half - j)
            return carry

        lax.fori_loop(0, pairs, give_one, 0)
        lax.fori_loop(0, pairs, keep_one, 0)
        lax.fori_loop(0, half, ring_one, 0)
    for i in range(reqs):
        right_copy(0, i).wait_recv()
        left_copy(0, i).wait_recv()
        value = csum[chip % pairs, chip // pairs, i]
        value = value + rrecv[0, i].astype(jnp.float32) + lrecv[0, i].astype(jnp.float32)
        out_ref[i] = (xg[me, i].astype(jnp.float32) + value).astype(jnp.bfloat16)

    def ring_sent(t, carry):
        for i in range(reqs):
            right_copy(t, i).wait_send()
            left_copy(t, i).wait_send()
        return carry

    lax.fori_loop(0, half - 1, ring_sent, 0)
    for i in range(reqs):
        (right_copy if goes_right(i) else left_copy)(half - 1, i).wait_send()

    def pair_sent(k, carry):
        pair_copy(k).wait_send()
        return carry

    lax.fori_loop(0, pairs, pair_sent, 0)

    def gather_sent(t, carry):
        for i in range(reqs):
            to_right(chip_at(-t) * CORES + core, i).wait_send()
            to_pair(chip_at(-t) * CORES + core, i).wait_send()
            to_left(chip_at(t) * CORES + core, i).wait_send()
            to_pair(chip_at(t) * CORES + core, i).wait_send()
        return carry

    for i in range(reqs):
        to_right(me, i).wait_send()
        to_left(me, i).wait_send()
        to_pair(me, i).wait_send()
        to_pair(far_chip * CORES + core, i).wait_send()
        (to_right(chip_at(1 - half) * CORES + core, i) if goes_right(i) else to_left(
            chip_at(half - 1) * CORES + core, i
        )).wait_send()
        to_pair(chip_at(1 - half) * CORES + core, i).wait_send()
        to_pair(chip_at(half - 1) * CORES + core, i).wait_send()
    lax.fori_loop(1, half - 1, gather_sent, 0)


def body(
    snake,
    queries,
    block_kv,
    cache_kv,
    prefix_len,
    block_valid,
    resid,
    norm_gain,
    w_gate,
    w_up,
    w_down,
):
    count = lax.axis_size("ffn")
    ring = count // CORES
    half = ring // 2
    _, reqs, block_len, width = queries.shape
    hidden_here = w_gate.shape[1]
    groups = count // KVH
    rows = reqs * block_len
    pairs = KVH // CORES
    lanes = block_kv.shape[3] // 2
    bf16, f32 = jnp.bfloat16, jnp.float32
    vmem = pl.BlockSpec(memory_space=pltpu.VMEM)
    smem = pl.BlockSpec(memory_space=pltpu.SMEM)
    hbm = pl.BlockSpec(memory_space=pl.ANY)
    dma = pltpu.SemaphoreType.DMA
    flops = 2 * groups * rows * KVH * width * hidden_here * 3
    out = pl.pallas_call(
        functools.partial(layer_kernel, ring, snake),
        out_shape=jax.ShapeDtypeStruct((reqs, block_len, width), bf16),
        in_specs=[vmem, vmem, hbm, smem, smem, vmem, vmem, hbm, hbm, hbm],
        out_specs=vmem,
        scratch_shapes=[
            pltpu.VMEM(cache_kv.shape[1:], bf16),
            pltpu.VMEM(w_gate.shape, bf16),
            pltpu.VMEM(w_up.shape, bf16),
            pltpu.VMEM(w_down.shape, bf16),
            pltpu.VMEM((count, reqs, block_len, width), bf16),
            pltpu.VMEM((groups * rows, hidden_here), f32),
            pltpu.VMEM((groups * rows, hidden_here), f32),
            pltpu.VMEM((groups * rows, lanes), f32),
            pltpu.VMEM((groups * rows, hidden_here), bf16),
            pltpu.VMEM((pairs, groups, reqs, block_len, width), f32),
            pltpu.VMEM((pairs, groups, reqs, block_len, width), bf16),
            pltpu.VMEM((pairs, groups, reqs, block_len, width), bf16),
            pltpu.VMEM((half, reqs, block_len, width), bf16),
            pltpu.VMEM((half, reqs, block_len, width), bf16),
            pltpu.VMEM((half, reqs, block_len, width), bf16),
            pltpu.VMEM((half, reqs, block_len, width), bf16),
            dma((reqs,)),
            dma((3, KVH)),
            dma((count, reqs)),
            dma((count, reqs)),
            dma((count, reqs)),
            dma((count, reqs)),
            dma((pairs,)),
            dma((pairs,)),
            dma((half, reqs)),
            dma((half, reqs)),
            dma((half, reqs)),
            dma((half, reqs)),
        ],
        compiler_params=pltpu.CompilerParams(
            collective_id=0, has_side_effects=True, vmem_limit_bytes=57 * 1024 * 1024
        ),
        cost_estimate=pl.CostEstimate(
            flops=flops, bytes_accessed=6 * KVH * width * hidden_here, transcendentals=0
        ),
    )(
        queries[0],
        block_kv[0],
        cache_kv[0],
        prefix_len,
        block_valid,
        resid[0],
        norm_gain.reshape(1, -1),
        w_gate,
        w_up,
        w_down,
    )
    return out[None]


def solution(mesh):
    in_specs = (
        P(("groups", "ffn"), None, None, None),
        P(("groups", "ffn"), None, None, None),
        P(("groups", "ffn"), None, None, None),
        P("groups"),
        P("groups"),
        P(("groups", "ffn"), None, None, None),
        P(),
        P(None, "ffn"),
        P(None, "ffn"),
        P("ffn", None),
    )
    out_specs = P(("groups", "ffn"), None, None, None)
    return jax.shard_map(
        functools.partial(body, ring_is_snake(mesh)),
        mesh=mesh,
        in_specs=in_specs,
        out_specs=out_specs,
        check_vma=False,
    )
```

```python
import functools
import math

import jax
import jax.numpy as jnp
from jax import lax
from jax.experimental import pallas as pl
from jax.experimental.pallas import tpu as pltpu
from jax.sharding import PartitionSpec as P

KVH = 8
CORES = 2

epsilon = 1e-05


def ring_is_snake(mesh):
    row = mesh.devices.reshape(mesh.shape["groups"], mesh.shape["ffn"])[0]
    chips = [getattr(row[i], "coords", None) for i in range(0, len(row), CORES)]
    if len(chips) < 4 or any(c is None for c in chips):
        return False
    return any(
        all(c[axis] == chips[i % 2][axis] for i, c in enumerate(chips))
        and chips[0][axis] != chips[1][axis]
        for axis in range(len(chips[0]))
    )


def layer_kernel(
    ring,
    snake,
    q_ref,
    bkv_ref,
    cache_hbm,
    prefix_ref,
    valid_ref,
    resid_ref,
    gain_ref,
    wg_hbm,
    wu_hbm,
    wd_hbm,
    out_ref,
    cache,
    wg,
    wu,
    wd,
    xg,
    acc_g,
    acc_u,
    sumsq,
    hid,
    csum,
    psend,
    precv,
    rsend,
    rrecv,
    lsend,
    lrecv,
    cache_sem,
    w_sem,
    ag_recv,
    ag_right,
    ag_left,
    ag_pair,
    p_ssem,
    p_rsem,
    r_ssem,
    r_rsem,
    l_ssem,
    l_rsem,
):
    reqs, block_len, width = q_ref.shape
    cache_len = cache.shape[1]
    head_size = cache.shape[2] // 2
    heads = width // head_size
    hidden_here = wg.shape[1]
    model_width = KVH * width
    rows = reqs * block_len
    groups = acc_g.shape[0] // rows
    pieces, piece_len = xg.shape[1:3]
    splits = pieces // reqs
    pairs = KVH // CORES
    half = ring // 2
    paired = snake and ring == 2 * pairs == 8 and groups == 2
    me = lax.axis_index("ffn")
    core = me % CORES
    chip = me // CORES
    if snake:
        here = (1 - chip % 2) * (chip // 2) + (chip % 2) * (ring - 1 - chip // 2)
    else:
        here = chip

    def chip_at(offset):
        place = (here + offset + ring) % ring
        if not snake:
            return place
        back = place // half
        return (1 - back) * (2 * place) + back * (2 * (ring - 1 - place) + 1)

    partner = chip * CORES + (1 - core)
    right = chip_at(1) * CORES + core
    left = chip_at(-1) * CORES + core

    barrier = pltpu.get_barrier_semaphore()
    for other in (partner, right, left):
        pl.semaphore_signal(
            barrier, inc=1, device_id={"ffn": other}, device_id_type=pl.DeviceIdType.MESH
        )

    def cache_copy(r):
        return pltpu.make_async_copy(cache_hbm.at[r], cache.at[r], cache_sem.at[r])

    for r in range(reqs):
        cache_copy(r).start()

    def flipped(bits):
        low = (chip + bits) % 2
        high = (chip // 2 + bits // 2) % 2
        return 2 * high + low

    far_chip = chip_at(half)
    other = 1 - core

    def gate_copy(h):
        span = pl.ds(pl.multiple_of(h * width, width), width)
        return pltpu.make_async_copy(wg_hbm.at[span], wg.at[span], w_sem.at[0, h])

    def up_copy(h):
        span = pl.ds(pl.multiple_of(h * width, width), width)
        return pltpu.make_async_copy(wu_hbm.at[span], wu.at[span], w_sem.at[1, h])

    def down_copy(h):
        span = pl.ds(pl.multiple_of(h * width, width), width)
        return pltpu.make_async_copy(wd_hbm.at[:, span], wd.at[:, span], w_sem.at[2, h])

    def head_at(step):
        return flipped(step // CORES) * CORES + step % CORES if paired else step

    def start_gate_up(step, carry):
        gate_copy(head_at(step)).start()
        up_copy(head_at(step)).start()
        return carry

    def wait_gate_up(step, carry):
        gate_copy(head_at(step)).wait()
        up_copy(head_at(step)).wait()
        return carry

    def start_down(j, carry):
        @pl.when(j < pairs)
        def _():
            down_copy(give_chip(j) * CORES + other).start()

        @pl.when(j > 0)
        def _():
            down_copy(give_chip(j - 1) * CORES + core).start()

        return carry

    def give_chip(j):
        return flipped(pairs - 1 - j) if paired else j

    def send(source, target, ssem, rsem, device):
        return pltpu.make_async_remote_copy(
            src_ref=source,
            dst_ref=target,
            send_sem=ssem,
            recv_sem=rsem,
            device_id={"ffn": device},
            device_id_type=pl.DeviceIdType.MESH,
        )

    def to_right(s, i):
        return send(xg.at[s, i], xg.at[s, i], ag_right.at[s, i], ag_recv.at[s, i], right)

    def to_left(s, i):
        return send(xg.at[s, i], xg.at[s, i], ag_left.at[s, i], ag_recv.at[s, i], left)

    def to_pair(s, i):
        return send(xg.at[s, i], xg.at[s, i], ag_pair.at[s, i], ag_recv.at[s, i], partner)

    def goes_right(i):
        return i < pieces // 2

    group = me // KVH
    scale = math.log2(math.e) / (head_size**0.5)
    parts = 2 if heads % 2 == 0 else 1
    part_heads = heads // parts
    part_width = part_heads * head_size

    def attend(step, carry):
        r = step // parts
        part = step % parts

        @pl.when(step == 0)
        def _():
            for i in range(reqs):
                cache_copy(i).wait()
            lax.fori_loop(0, KVH, start_gate_up, 0)

        columns = pl.ds(pl.multiple_of(part * part_width, part_width), part_width)
        query = q_ref[r, :, columns]
        stacked = jnp.concatenate(
            [query[:, h * head_size : (h + 1) * head_size] for h in range(part_heads)], axis=0
        )
        contract = (((1,), (1,)), ((), ()))
        far = lax.dot_general(
            stacked, cache[r, :, :head_size], contract, preferred_element_type=jnp.float32
        )
        near = lax.dot_general(
            stacked, bkv_ref[r, :, :head_size], contract, preferred_element_type=jnp.float32
        )
        seen = prefix_ref[group * reqs + r]
        live = valid_ref[group * reqs + r]
        far_at = lax.broadcasted_iota(jnp.int32, (1, cache_len), 1)
        near_at = lax.broadcasted_iota(jnp.int32, (1, block_len), 1)
        far = jnp.where(far_at < seen, far, -1e30)
        near = jnp.where(near_at < live, near, -1e30)
        peak = jnp.maximum(
            jnp.max(far, axis=-1, keepdims=True), jnp.max(near, axis=-1, keepdims=True)
        )
        far = jnp.exp2((far - peak) * scale)
        near = jnp.exp2((near - peak) * scale)
        total = jnp.sum(far, axis=-1, keepdims=True) + jnp.sum(near, axis=-1, keepdims=True)
        inverse = 1.0 / total
        mixed = jnp.dot(
            (far * inverse).astype(jnp.bfloat16),
            cache[r, :, head_size:],
            preferred_element_type=jnp.float32,
        ) + jnp.dot(
            (near * inverse).astype(jnp.bfloat16),
            bkv_ref[r, :, head_size:],
            preferred_element_type=jnp.float32,
        )
        side = jnp.concatenate(
            [mixed[h * block_len : (h + 1) * block_len] for h in range(part_heads)], axis=1
        )
        state = resid_ref[r, :, columns].astype(jnp.float32) + side
        for piece in range(splits):
            xg[me, r * splits + piece, :, columns] = state[
                piece * piece_len : (piece + 1) * piece_len
            ].astype(jnp.bfloat16)

        @pl.when(step == parts - 1)
        def _():
            pl.semaphore_wait(barrier, 3)

        @pl.when(part == parts - 1)
        def _():
            for piece in range(splits):
                i = r * splits + piece
                to_right(me, i).start()
                to_left(me, i).start()
                to_pair(me, i).start()

        return carry

    lax.fori_loop(0, reqs * parts, attend, 0)

    def fold(square):
        folded = square[:, :head_size]
        for h in range(1, square.shape[1] // head_size):
            folded = folded + square[:, h * head_size : (h + 1) * head_size]
        return folded

    def absorb(s):
        mine = pl.ds(pl.multiple_of((s // KVH) * rows, rows), rows)
        span = pl.ds(pl.multiple_of((s % KVH) * width, width), width)
        block = xg[s].reshape(rows, width).astype(jnp.float32)
        sumsq[mine] += fold(block * block)
        scaled = (block * gain_ref[:, span]).astype(jnp.bfloat16)
        acc_g[mine] += jnp.dot(scaled, wg[span, :], preferred_element_type=jnp.float32)
        acc_u[mine] += jnp.dot(scaled, wu[span, :], preferred_element_type=jnp.float32)

    def absorb_head(h):
        span = pl.ds(pl.multiple_of(h * width, width), width)
        block = jnp.concatenate(
            [xg[g * KVH + h].reshape(rows, width) for g in range(groups)], axis=0
        ).astype(jnp.float32)
        sumsq[...] += fold(block * block)
        scaled = (block * gain_ref[:, span]).astype(jnp.bfloat16)
        acc_g[...] += jnp.dot(scaled, wg[span, :], preferred_element_type=jnp.float32)
        acc_u[...] += jnp.dot(scaled, wu[span, :], preferred_element_type=jnp.float32)

    def pair_arrived(s):
        for i in range(pieces):
            to_pair(s, i).wait_recv()

    def absorb_pair(s):
        pair_arrived(s)
        absorb(s)

    def pass_on(t, last):
        from_left = chip_at(-t) * CORES + core
        from_right = chip_at(t) * CORES + core
        for i in range(pieces):
            to_right(from_left, i).wait_recv()
            if not last or goes_right(i):
                to_right(from_left, i).start()
            to_pair(from_left, i).start()
            to_left(from_right, i).wait_recv()
            if not last or not goes_right(i):
                to_left(from_right, i).start()
            to_pair(from_right, i).start()

    def absorb_step(t):
        absorb(chip_at(-t) * CORES + core)
        absorb(chip_at(t) * CORES + core)
        absorb_pair(chip_at(-t) * CORES + 1 - core)
        absorb_pair(chip_at(t) * CORES + 1 - core)

    def from_far():
        for i in range(pieces):
            (to_right if goes_right(i) else to_left)(far_chip * CORES + core, i).wait_recv()
            to_pair(far_chip * CORES + core, i).start()

    acc_g[...] = jnp.zeros_like(acc_g)
    acc_u[...] = jnp.zeros_like(acc_u)
    sumsq[...] = jnp.zeros_like(sumsq)

    if paired:
        def from_both(t):
            pair_arrived(chip_at(-t) * CORES + other)
            pair_arrived(chip_at(t) * CORES + other)

        pass_on(1, False)
        pair_arrived(partner)
        pass_on(2, False)
        lax.fori_loop(0, pairs + 1, start_down, 0)
        from_both(1)
        from_both(2)

        def stage(step, carry):
            @pl.when(step == 1)
            def _():
                pass_on(3, True)

            @pl.when(step == CORES)
            def _():
                from_both(3)

            @pl.when(step == CORES + 1)
            def _():
                from_far()

            @pl.when(step == 3 * CORES)
            def _():
                pair_arrived(far_chip * CORES + other)

            wait_gate_up(step, 0)
            absorb_head(head_at(step))
            return carry

        lax.fori_loop(0, KVH, stage, 0)
    else:
        pass_on(1, half == 2)
        lax.fori_loop(0, pairs + 1, start_down, 0)
        lax.fori_loop(0, KVH, wait_gate_up, 0)
        absorb(me)
        absorb_pair(partner)
        absorb_step(1)

        def middle(t, carry):
            pass_on(t, False)
            absorb_step(t)
            return carry

        if half > 2:
            lax.fori_loop(2, half - 1, middle, 0)
            pass_on(half - 1, True)
            absorb_step(half - 1)
        from_far()
        absorb(far_chip * CORES + core)
        absorb_pair(far_chip * CORES + other)

    mean_square = jnp.sum(sumsq[...], axis=-1, keepdims=True) / model_width
    root = lax.rsqrt(mean_square + epsilon)
    gate = acc_g[...] * root
    up = acc_u[...] * root
    hid[...] = (gate * jax.nn.sigmoid(gate) * up).astype(jnp.bfloat16)

    def pair_copy(k):
        return send(psend.at[k], precv.at[k], p_ssem.at[k], p_rsem.at[k], partner)

    def column_of(k, parity):
        return pl.ds(pl.multiple_of((k * CORES + parity) * width, width), width)

    def give(k):
        down_copy(k * CORES + other).wait()
        share = jnp.dot(hid[...], wd[:, column_of(k, other)], preferred_element_type=jnp.float32)
        psend[k] = share.astype(jnp.bfloat16).reshape(groups, pieces, piece_len, width)
        pair_copy(k).start()

    def keep(k):
        down_copy(k * CORES + core).wait()
        share = jnp.dot(hid[...], wd[:, column_of(k, core)], preferred_element_type=jnp.float32)
        pair_copy(k).wait_recv()
        csum[k] = share.reshape(groups, pieces, piece_len, width) + precv[k].astype(jnp.float32)

    def right_copy(t, i):
        return send(rsend.at[t, i], rrecv.at[t, i], r_ssem.at[t, i], r_rsem.at[t, i], right)

    def left_copy(t, i):
        return send(lsend.at[t, i], lrecv.at[t, i], l_ssem.at[t, i], l_rsem.at[t, i], left)

    def ring_move(t, i, first, copy_of, out_buf, in_buf, offset):
        target = chip_at(offset)

        def own():
            return csum[target % pairs, target // pairs, i]

        fed = (t < half - 1) | ((t == half - 1) & first)

        @pl.when(fed)
        def _():
            copy_of(t, i).wait_recv()
            total = own() + in_buf[t, i].astype(jnp.float32)
            out_buf[t - 1, i] = total.astype(jnp.bfloat16)

        @pl.when(jnp.logical_not(fed))
        def _():
            out_buf[t - 1, i] = own().astype(jnp.bfloat16)

        copy_of(t - 1, i).start()

    def ring_step(t):
        def piece(i, carry):
            late = i >= pieces // 2

            @pl.when((t < half) | late)
            def _():
                ring_move(t, pieces - 1 - i, late, right_copy, rsend, rrecv, t)
                ring_move(t, i, late, left_copy, lsend, lrecv, -t)

            return carry

        lax.fori_loop(0, pieces, piece, 0)

    if paired:
        def down(j, carry):
            @pl.when(j < pairs)
            def _():
                give(give_chip(j))

            @pl.when((j > 0) & (j <= pairs))
            def _():
                keep(give_chip(j - 1))

            @pl.when((j == 1) | (j > 2))
            def _():
                ring_step(jnp.minimum(half, half + 2 - j))

            return carry

        lax.fori_loop(0, pairs + 2, down, 0)
    else:

        def give_one(j, carry):
            give(j)
            return carry

        def keep_one(j, carry):
            keep(j)
            return carry

        def ring_one(j, carry):
            ring_step(half - j)
            return carry

        lax.fori_loop(0, pairs, give_one, 0)
        lax.fori_loop(0, pairs, keep_one, 0)
        lax.fori_loop(0, half, ring_one, 0)
    for i in range(pieces):
        right_copy(0, i).wait_recv()
        left_copy(0, i).wait_recv()
        value = csum[chip % pairs, chip // pairs, i]
        value = value + rrecv[0, i].astype(jnp.float32) + lrecv[0, i].astype(jnp.float32)
        within = pl.ds(i % splits * piece_len, piece_len)
        out_ref[i // splits, within] = (xg[me, i].astype(jnp.float32) + value).astype(jnp.bfloat16)

    def ring_sent(t, carry):
        for i in range(pieces):
            right_copy(t, i).wait_send()
            left_copy(t, i).wait_send()
        return carry

    lax.fori_loop(0, half - 1, ring_sent, 0)
    for i in range(pieces):
        (right_copy if goes_right(i) else left_copy)(half - 1, i).wait_send()

    def pair_sent(k, carry):
        pair_copy(k).wait_send()
        return carry

    lax.fori_loop(0, pairs, pair_sent, 0)

    def gather_sent(t, carry):
        for i in range(pieces):
            to_right(chip_at(-t) * CORES + core, i).wait_send()
            to_pair(chip_at(-t) * CORES + core, i).wait_send()
            to_left(chip_at(t) * CORES + core, i).wait_send()
            to_pair(chip_at(t) * CORES + core, i).wait_send()
        return carry

    for i in range(pieces):
        to_right(me, i).wait_send()
        to_left(me, i).wait_send()
        to_pair(me, i).wait_send()
        to_pair(far_chip * CORES + core, i).wait_send()
        (to_right(chip_at(1 - half) * CORES + core, i) if goes_right(i) else to_left(
            chip_at(half - 1) * CORES + core, i
        )).wait_send()
        to_pair(chip_at(1 - half) * CORES + core, i).wait_send()
        to_pair(chip_at(half - 1) * CORES + core, i).wait_send()
    lax.fori_loop(1, half - 1, gather_sent, 0)


def body(
    snake,
    queries,
    block_kv,
    cache_kv,
    prefix_len,
    block_valid,
    resid,
    norm_gain,
    w_gate,
    w_up,
    w_down,
):
    count = lax.axis_size("ffn")
    ring = count // CORES
    half = ring // 2
    _, reqs, block_len, width = queries.shape
    hidden_here = w_gate.shape[1]
    groups = count // KVH
    rows = reqs * block_len
    pairs = KVH // CORES
    lanes = block_kv.shape[3] // 2
    splits = 2 if block_len % 32 == 0 else 1
    pieces, piece_len = reqs * splits, block_len // splits
    bf16, f32 = jnp.bfloat16, jnp.float32
    vmem = pl.BlockSpec(memory_space=pltpu.VMEM)
    smem = pl.BlockSpec(memory_space=pltpu.SMEM)
    hbm = pl.BlockSpec(memory_space=pl.ANY)
    dma = pltpu.SemaphoreType.DMA
    flops = 2 * groups * rows * KVH * width * hidden_here * 3
    out = pl.pallas_call(
        functools.partial(layer_kernel, ring, snake),
        out_shape=jax.ShapeDtypeStruct((reqs, block_len, width), bf16),
        in_specs=[vmem, vmem, hbm, smem, smem, vmem, vmem, hbm, hbm, hbm],
        out_specs=vmem,
        scratch_shapes=[
            pltpu.VMEM(cache_kv.shape[1:], bf16),
            pltpu.VMEM(w_gate.shape, bf16),
            pltpu.VMEM(w_up.shape, bf16),
            pltpu.VMEM(w_down.shape, bf16),
            pltpu.VMEM((count, pieces, piece_len, width), bf16),
            pltpu.VMEM((groups * rows, hidden_here), f32),
            pltpu.VMEM((groups * rows, hidden_here), f32),
            pltpu.VMEM((groups * rows, lanes), f32),
            pltpu.VMEM((groups * rows, hidden_here), bf16),
            pltpu.VMEM((pairs, groups, pieces, piece_len, width), f32),
            pltpu.VMEM((pairs, groups, pieces, piece_len, width), bf16),
            pltpu.VMEM((pairs, groups, pieces, piece_len, width), bf16),
            pltpu.VMEM((half, pieces, piece_len, width), bf16),
            pltpu.VMEM((half, pieces, piece_len, width), bf16),
            pltpu.VMEM((half, pieces, piece_len, width), bf16),
            pltpu.VMEM((half, pieces, piece_len, width), bf16),
            dma((reqs,)),
            dma((3, KVH)),
            dma((count, pieces)),
            dma((count, pieces)),
            dma((count, pieces)),
            dma((count, pieces)),
            dma((pairs,)),
            dma((pairs,)),
            dma((half, pieces)),
            dma((half, pieces)),
            dma((half, pieces)),
            dma((half, pieces)),
        ],
        compiler_params=pltpu.CompilerParams(
            collective_id=0, has_side_effects=True, vmem_limit_bytes=57 * 1024 * 1024
        ),
        cost_estimate=pl.CostEstimate(
            flops=flops, bytes_accessed=6 * KVH * width * hidden_here, transcendentals=0
        ),
    )(
        queries[0],
        block_kv[0],
        cache_kv[0],
        prefix_len,
        block_valid,
        resid[0],
        norm_gain.reshape(1, -1),
        w_gate,
        w_up,
        w_down,
    )
    return out[None]


def solution(mesh):
    in_specs = (
        P(("groups", "ffn"), None, None, None),
        P(("groups", "ffn"), None, None, None),
        P(("groups", "ffn"), None, None, None),
        P("groups"),
        P("groups"),
        P(("groups", "ffn"), None, None, None),
        P(),
        P(None, "ffn"),
        P(None, "ffn"),
        P("ffn", None),
    )
    out_specs = P(("groups", "ffn"), None, None, None)
    return jax.shard_map(
        functools.partial(body, ring_is_snake(mesh)),
        mesh=mesh,
        in_specs=in_specs,
        out_specs=out_specs,
        check_vma=False,
    )
```

```python
import functools
import math

import jax
import jax.numpy as jnp
from jax import lax
from jax.experimental import pallas as pl
from jax.experimental.pallas import tpu as pltpu
from jax.sharding import PartitionSpec as P

KVH = 8
CORES = 2

epsilon = 1e-05


def ring_is_snake(mesh):
    row = mesh.devices.reshape(mesh.shape["groups"], mesh.shape["ffn"])[0]
    chips = [getattr(row[i], "coords", None) for i in range(0, len(row), CORES)]
    if len(chips) < 4 or any(c is None for c in chips):
        return False
    return any(
        all(c[axis] == chips[i % 2][axis] for i, c in enumerate(chips))
        and chips[0][axis] != chips[1][axis]
        for axis in range(len(chips[0]))
    )


def layer_kernel(
    ring,
    snake,
    q_hbm,
    bkv_hbm,
    cache_hbm,
    prefix_ref,
    valid_ref,
    resid_hbm,
    gain_hbm,
    wg_hbm,
    wu_hbm,
    wd_hbm,
    out_ref,
    q_ref,
    bkv_ref,
    resid_ref,
    gain_ref,
    cache,
    wg,
    wu,
    wd,
    xg,
    acc_g,
    acc_u,
    sumsq,
    hid,
    csum,
    psend,
    precv,
    rsend,
    rrecv,
    lsend,
    lrecv,
    in_sem,
    cache_sem,
    w_sem,
    ag_recv,
    ag_right,
    ag_left,
    ag_pair,
    ag_pair_recv,
    p_ssem,
    p_rsem,
    r_ssem,
    r_rsem,
    l_ssem,
    l_rsem,
):
    reqs, block_len, width = q_ref.shape
    cache_len = cache.shape[1]
    head_size = cache.shape[2] // 2
    heads = width // head_size
    hidden_here = wg.shape[1]
    model_width = KVH * width
    rows = reqs * block_len
    groups = acc_g.shape[0] // rows
    pieces = xg.shape[1]
    part_width = xg.shape[3]
    parts = pieces // reqs
    part_heads = part_width // head_size
    pairs = KVH // CORES
    half = ring // 2
    paired = snake and ring == 2 * pairs == 8 and groups == 2
    me = lax.axis_index("ffn")
    core = me % CORES
    chip = me // CORES
    if snake:
        here = (1 - chip % 2) * (chip // 2) + (chip % 2) * (ring - 1 - chip // 2)
    else:
        here = chip

    def chip_at(offset):
        place = (here + offset + ring) % ring
        if not snake:
            return place
        back = place // half
        return (1 - back) * (2 * place) + back * (2 * (ring - 1 - place) + 1)

    partner = chip * CORES + (1 - core)
    right = chip_at(1) * CORES + core
    left = chip_at(-1) * CORES + core

    barrier = pltpu.get_barrier_semaphore()
    for other in (partner, right, left):
        pl.semaphore_signal(
            barrier, inc=1, device_id={"ffn": other}, device_id_type=pl.DeviceIdType.MESH
        )

    def cache_copy(r):
        return pltpu.make_async_copy(cache_hbm.at[r], cache.at[r], cache_sem.at[r])

    small_copies = [
        pltpu.make_async_copy(source, target, in_sem.at[n])
        for n, (source, target) in enumerate(
            ((q_hbm, q_ref), (bkv_hbm, bkv_ref), (resid_hbm, resid_ref), (gain_hbm, gain_ref))
        )
    ]
    for copy in small_copies:
        copy.start()
    for r in range(reqs):
        cache_copy(r).start()

    def flipped(bits):
        low = (chip + bits) % 2
        high = (chip // 2 + bits // 2) % 2
        return 2 * high + low

    far_chip = chip_at(half)
    other = 1 - core

    def gate_copy(h):
        span = pl.ds(pl.multiple_of(h * width, width), width)
        return pltpu.make_async_copy(wg_hbm.at[span], wg.at[span], w_sem.at[0, h])

    def up_copy(h):
        span = pl.ds(pl.multiple_of(h * width, width), width)
        return pltpu.make_async_copy(wu_hbm.at[span], wu.at[span], w_sem.at[1, h])

    def down_copy(h):
        span = pl.ds(pl.multiple_of(h * width, width), width)
        return pltpu.make_async_copy(wd_hbm.at[:, span], wd.at[:, span], w_sem.at[2, h])

    def head_at(step):
        return flipped(step // CORES) * CORES + step % CORES if paired else step

    def start_gate_up(step, carry):
        gate_copy(head_at(step)).start()
        up_copy(head_at(step)).start()
        return carry

    def wait_gate_up(step, carry):
        gate_copy(head_at(step)).wait()
        up_copy(head_at(step)).wait()
        return carry

    def start_down(j, carry):
        @pl.when(j < pairs)
        def _():
            down_copy(give_chip(j) * CORES + other).start()

        @pl.when(j > 0)
        def _():
            down_copy(give_chip(j - 1) * CORES + core).start()

        return carry

    def give_chip(j):
        return flipped(pairs - 1 - j) if paired else j

    def send(source, target, ssem, rsem, device):
        return pltpu.make_async_remote_copy(
            src_ref=source,
            dst_ref=target,
            send_sem=ssem,
            recv_sem=rsem,
            device_id={"ffn": device},
            device_id_type=pl.DeviceIdType.MESH,
        )

    def to_right(s, i):
        return send(xg.at[s, i], xg.at[s, i], ag_right.at[s, i], ag_recv.at[s, i], right)

    def to_left(s, i):
        return send(xg.at[s, i], xg.at[s, i], ag_left.at[s, i], ag_recv.at[s, i], left)

    def to_pair(s):
        return send(xg.at[s], xg.at[s], ag_pair.at[s], ag_pair_recv.at[s], partner)

    def goes_right(i):
        return i < pieces // 2

    group = me // KVH
    scale = math.log2(math.e) / (head_size**0.5)
    for copy in small_copies:
        copy.wait()
    for r in range(reqs):
        cache_copy(r).wait()
    lax.fori_loop(0, KVH, start_gate_up, 0)

    def attend(step, carry):
        r = step // parts
        part = step % parts

        columns = pl.ds(pl.multiple_of(part * part_width, part_width), part_width)
        query = q_ref[r, :, columns]
        stacked = jnp.concatenate(
            [query[:, h * head_size : (h + 1) * head_size] for h in range(part_heads)], axis=0
        )
        contract = (((1,), (1,)), ((), ()))
        far = lax.dot_general(
            stacked, cache[r, :, :head_size], contract, preferred_element_type=jnp.float32
        )
        near = lax.dot_general(
            stacked, bkv_ref[r, :, :head_size], contract, preferred_element_type=jnp.float32
        )
        seen = prefix_ref[group * reqs + r]
        live = valid_ref[group * reqs + r]
        far_at = lax.broadcasted_iota(jnp.int32, (1, cache_len), 1)
        near_at = lax.broadcasted_iota(jnp.int32, (1, block_len), 1)
        far = jnp.where(far_at < seen, far, -1e30)
        near = jnp.where(near_at < live, near, -1e30)
        peak = jnp.maximum(
            jnp.max(far, axis=-1, keepdims=True), jnp.max(near, axis=-1, keepdims=True)
        )
        far = jnp.exp2((far - peak) * scale)
        near = jnp.exp2((near - peak) * scale)
        total = jnp.sum(far, axis=-1, keepdims=True) + jnp.sum(near, axis=-1, keepdims=True)
        inverse = 1.0 / total
        mixed = jnp.dot(
            (far * inverse).astype(jnp.bfloat16),
            cache[r, :, head_size:],
            preferred_element_type=jnp.float32,
        ) + jnp.dot(
            (near * inverse).astype(jnp.bfloat16),
            bkv_ref[r, :, head_size:],
            preferred_element_type=jnp.float32,
        )
        side = jnp.concatenate(
            [mixed[h * block_len : (h + 1) * block_len] for h in range(part_heads)], axis=1
        )
        state = resid_ref[r, :, columns].astype(jnp.float32) + side
        xg[me, step] = state.astype(jnp.bfloat16)

        @pl.when(step == 0)
        def _():
            pl.semaphore_wait(barrier, 3)

        to_right(me, step).start()
        to_left(me, step).start()
        return carry

    lax.fori_loop(0, pieces, attend, 0)
    to_pair(me).start()

    def block_of(s):
        return jnp.concatenate(
            [
                jnp.concatenate([xg[s, r * parts + part] for part in range(parts)], axis=1)
                for r in range(reqs)
            ],
            axis=0,
        )

    def fold(square):
        folded = square[:, :head_size]
        for h in range(1, square.shape[1] // head_size):
            folded = folded + square[:, h * head_size : (h + 1) * head_size]
        return folded

    def absorb(s):
        mine = pl.ds(pl.multiple_of((s // KVH) * rows, rows), rows)
        span = pl.ds(pl.multiple_of((s % KVH) * width, width), width)
        block = block_of(s).astype(jnp.float32)
        sumsq[mine] += fold(block * block)
        scaled = (block * gain_ref[:, span]).astype(jnp.bfloat16)
        acc_g[mine] += jnp.dot(scaled, wg[span, :], preferred_element_type=jnp.float32)
        acc_u[mine] += jnp.dot(scaled, wu[span, :], preferred_element_type=jnp.float32)

    def absorb_head(h):
        span = pl.ds(pl.multiple_of(h * width, width), width)
        block = jnp.concatenate(
            [block_of(g * KVH + h) for g in range(groups)], axis=0
        ).astype(jnp.float32)
        sumsq[...] += fold(block * block)
        scaled = (block * gain_ref[:, span]).astype(jnp.bfloat16)
        acc_g[...] += jnp.dot(scaled, wg[span, :], preferred_element_type=jnp.float32)
        acc_u[...] += jnp.dot(scaled, wu[span, :], preferred_element_type=jnp.float32)

    def pair_arrived(s):
        to_pair(s).wait_recv()

    def absorb_pair(s):
        pair_arrived(s)
        absorb(s)

    def pass_on(t, last):
        from_left = chip_at(-t) * CORES + core
        from_right = chip_at(t) * CORES + core
        for i in range(pieces):
            to_right(from_left, i).wait_recv()
            if not last or goes_right(i):
                to_right(from_left, i).start()
            to_left(from_right, i).wait_recv()
            if not last or not goes_right(i):
                to_left(from_right, i).start()
        to_pair(from_left).start()
        to_pair(from_right).start()

    def absorb_step(t):
        absorb(chip_at(-t) * CORES + core)
        absorb(chip_at(t) * CORES + core)
        absorb_pair(chip_at(-t) * CORES + 1 - core)
        absorb_pair(chip_at(t) * CORES + 1 - core)

    def from_far():
        for i in range(pieces):
            (to_right if goes_right(i) else to_left)(far_chip * CORES + core, i).wait_recv()
        to_pair(far_chip * CORES + core).start()

    acc_g[...] = jnp.zeros_like(acc_g)
    acc_u[...] = jnp.zeros_like(acc_u)
    sumsq[...] = jnp.zeros_like(sumsq)

    if paired:
        def from_both(t):
            pair_arrived(chip_at(-t) * CORES + other)
            pair_arrived(chip_at(t) * CORES + other)

        pass_on(1, False)
        pair_arrived(partner)
        pass_on(2, False)
        lax.fori_loop(0, pairs + 1, start_down, 0)
        from_both(1)
        from_both(2)

        def stage(step, carry):
            @pl.when(step == 1)
            def _():
                pass_on(3, True)

            @pl.when(step == CORES)
            def _():
                from_both(3)

            @pl.when(step == CORES + 1)
            def _():
                from_far()

            @pl.when(step == 3 * CORES)
            def _():
                pair_arrived(far_chip * CORES + other)

            wait_gate_up(step, 0)
            absorb_head(head_at(step))
            return carry

        lax.fori_loop(0, KVH, stage, 0)
    else:
        pass_on(1, half == 2)
        lax.fori_loop(0, pairs + 1, start_down, 0)
        lax.fori_loop(0, KVH, wait_gate_up, 0)
        absorb(me)
        absorb_pair(partner)
        absorb_step(1)

        def middle(t, carry):
            pass_on(t, False)
            absorb_step(t)
            return carry

        if half > 2:
            lax.fori_loop(2, half - 1, middle, 0)
            pass_on(half - 1, True)
            absorb_step(half - 1)
        from_far()
        absorb(far_chip * CORES + core)
        absorb_pair(far_chip * CORES + other)

    mean_square = jnp.sum(sumsq[...], axis=-1, keepdims=True) / model_width
    root = lax.rsqrt(mean_square + epsilon)
    gate = acc_g[...] * root
    up = acc_u[...] * root
    hid[...] = (gate * jax.nn.sigmoid(gate) * up).astype(jnp.bfloat16)

    def pair_copy(k):
        return send(psend.at[k], precv.at[k], p_ssem.at[k], p_rsem.at[k], partner)

    def column_of(k, parity):
        return pl.ds(pl.multiple_of((k * CORES + parity) * width, width), width)

    cuts = []
    for g in range(groups):
        for i in range(pieces):
            top = g * rows + i // parts * block_len
            side = i % parts * part_width
            cuts.append((g, i, (slice(top, top + block_len), slice(side, side + part_width))))

    def give(k):
        down_copy(k * CORES + other).wait()
        share = jnp.dot(hid[...], wd[:, column_of(k, other)], preferred_element_type=jnp.float32)
        for g, i, cut in cuts:
            psend[k, g, i] = share[cut].astype(jnp.bfloat16)
        pair_copy(k).start()

    def keep(k):
        down_copy(k * CORES + core).wait()
        share = jnp.dot(hid[...], wd[:, column_of(k, core)], preferred_element_type=jnp.float32)
        pair_copy(k).wait_recv()
        for g, i, cut in cuts:
            csum[k, g, i] = share[cut] + precv[k, g, i].astype(jnp.float32)

    def right_copy(t, i):
        return send(rsend.at[t, i], rrecv.at[t, i], r_ssem.at[t, i], r_rsem.at[t, i], right)

    def left_copy(t, i):
        return send(lsend.at[t, i], lrecv.at[t, i], l_ssem.at[t, i], l_rsem.at[t, i], left)

    def ring_move(t, i, first, copy_of, out_buf, in_buf, offset):
        target = chip_at(offset)

        def own():
            return csum[target % pairs, target // pairs, i]

        fed = (t < half - 1) | ((t == half - 1) & first)

        @pl.when(fed)
        def _():
            copy_of(t, i).wait_recv()
            total = own() + in_buf[t, i].astype(jnp.float32)
            out_buf[t - 1, i] = total.astype(jnp.bfloat16)

        @pl.when(jnp.logical_not(fed))
        def _():
            out_buf[t - 1, i] = own().astype(jnp.bfloat16)

        copy_of(t - 1, i).start()

    def ring_step(t):
        def piece(i, carry):
            late = i >= pieces // 2

            @pl.when((t < half) | late)
            def _():
                ring_move(t, pieces - 1 - i, late, right_copy, rsend, rrecv, t)
                ring_move(t, i, late, left_copy, lsend, lrecv, -t)

            return carry

        lax.fori_loop(0, pieces, piece, 0)

    if paired:
        def down(j, carry):
            @pl.when(j < pairs)
            def _():
                give(give_chip(j))

            @pl.when((j > 0) & (j <= pairs))
            def _():
                keep(give_chip(j - 1))

            @pl.when((j == 1) | (j > 2))
            def _():
                ring_step(jnp.minimum(half, half + 2 - j))

            return carry

        lax.fori_loop(0, pairs + 2, down, 0)
    else:

        def give_one(j, carry):
            give(j)
            return carry

        def keep_one(j, carry):
            keep(j)
            return carry

        def ring_one(j, carry):
            ring_step(half - j)
            return carry

        lax.fori_loop(0, pairs, give_one, 0)
        lax.fori_loop(0, pairs, keep_one, 0)
        lax.fori_loop(0, half, ring_one, 0)
    for i in range(pieces):
        right_copy(0, i).wait_recv()
        left_copy(0, i).wait_recv()
        value = csum[chip % pairs, chip // pairs, i]
        value = value + rrecv[0, i].astype(jnp.float32) + lrecv[0, i].astype(jnp.float32)
        columns = pl.ds(i % parts * part_width, part_width)
        value = xg[me, i].astype(jnp.float32) + value
        out_ref[i // parts, :, columns] = value.astype(jnp.bfloat16)

    def ring_sent(t, carry):
        for i in range(pieces):
            right_copy(t, i).wait_send()
            left_copy(t, i).wait_send()
        return carry

    lax.fori_loop(0, half - 1, ring_sent, 0)
    for i in range(pieces):
        (right_copy if goes_right(i) else left_copy)(half - 1, i).wait_send()

    def pair_sent(k, carry):
        pair_copy(k).wait_send()
        return carry

    lax.fori_loop(0, pairs, pair_sent, 0)

    def gather_sent(t, carry):
        for i in range(pieces):
            to_right(chip_at(-t) * CORES + core, i).wait_send()
            to_left(chip_at(t) * CORES + core, i).wait_send()
        to_pair(chip_at(-t) * CORES + core).wait_send()
        to_pair(chip_at(t) * CORES + core).wait_send()
        return carry

    for i in range(pieces):
        to_right(me, i).wait_send()
        to_left(me, i).wait_send()
        if goes_right(i):
            to_right(chip_at(1 - half) * CORES + core, i).wait_send()
        else:
            to_left(chip_at(half - 1) * CORES + core, i).wait_send()
    for s in (me, *(chip_at(t) * CORES + core for t in (half, half - 1, 1 - half))):
        to_pair(s).wait_send()
    lax.fori_loop(1, half - 1, gather_sent, 0)


def body(
    snake,
    queries,
    block_kv,
    cache_kv,
    prefix_len,
    block_valid,
    resid,
    norm_gain,
    w_gate,
    w_up,
    w_down,
):
    count = lax.axis_size("ffn")
    ring = count // CORES
    half = ring // 2
    _, reqs, block_len, width = queries.shape
    hidden_here = w_gate.shape[1]
    groups = count // KVH
    rows = reqs * block_len
    pairs = KVH // CORES
    lanes = block_kv.shape[3] // 2
    parts = 2 if (width // lanes) % 2 == 0 else 1
    pieces, part_width = reqs * parts, width // parts
    bf16, f32 = jnp.bfloat16, jnp.float32
    vmem = pl.BlockSpec(memory_space=pltpu.VMEM)
    smem = pl.BlockSpec(memory_space=pltpu.SMEM)
    hbm = pl.BlockSpec(memory_space=pl.ANY)
    dma = pltpu.SemaphoreType.DMA
    flops = 2 * groups * rows * KVH * width * hidden_here * 3
    out = pl.pallas_call(
        functools.partial(layer_kernel, ring, snake),
        out_shape=jax.ShapeDtypeStruct((reqs, block_len, width), bf16),
        in_specs=[hbm, hbm, hbm, smem, smem, hbm, hbm, hbm, hbm, hbm],
        out_specs=vmem,
        scratch_shapes=[
            pltpu.VMEM(queries.shape[1:], bf16),
            pltpu.VMEM(block_kv.shape[1:], bf16),
            pltpu.VMEM(resid.shape[1:], bf16),
            pltpu.VMEM((1, norm_gain.shape[0]), f32),
            pltpu.VMEM(cache_kv.shape[1:], bf16),
            pltpu.VMEM(w_gate.shape, bf16),
            pltpu.VMEM(w_up.shape, bf16),
            pltpu.VMEM(w_down.shape, bf16),
            pltpu.VMEM((count, pieces, block_len, part_width), bf16),
            pltpu.VMEM((groups * rows, hidden_here), f32),
            pltpu.VMEM((groups * rows, hidden_here), f32),
            pltpu.VMEM((groups * rows, lanes), f32),
            pltpu.VMEM((groups * rows, hidden_here), bf16),
            pltpu.VMEM((pairs, groups, pieces, block_len, part_width), f32),
            pltpu.VMEM((pairs, groups, pieces, block_len, part_width), bf16),
            pltpu.VMEM((pairs, groups, pieces, block_len, part_width), bf16),
            pltpu.VMEM((half, pieces, block_len, part_width), bf16),
            pltpu.VMEM((half, pieces, block_len, part_width), bf16),
            pltpu.VMEM((half, pieces, block_len, part_width), bf16),
            pltpu.VMEM((half, pieces, block_len, part_width), bf16),
            dma((4,)),
            dma((reqs,)),
            dma((3, KVH)),
            dma((count, pieces)),
            dma((count, pieces)),
            dma((count, pieces)),
            dma((count,)),
            dma((count,)),
            dma((pairs,)),
            dma((pairs,)),
            dma((half, pieces)),
            dma((half, pieces)),
            dma((half, pieces)),
            dma((half, pieces)),
        ],
        compiler_params=pltpu.CompilerParams(
            collective_id=0, has_side_effects=True, vmem_limit_bytes=57 * 1024 * 1024
        ),
        cost_estimate=pl.CostEstimate(
            flops=flops, bytes_accessed=6 * KVH * width * hidden_here, transcendentals=0
        ),
    )(
        queries[0],
        block_kv[0],
        cache_kv[0],
        prefix_len,
        block_valid,
        resid[0],
        norm_gain.reshape(1, -1),
        w_gate,
        w_up,
        w_down,
    )
    return out[None]


def solution(mesh):
    in_specs = (
        P(("groups", "ffn"), None, None, None),
        P(("groups", "ffn"), None, None, None),
        P(("groups", "ffn"), None, None, None),
        P("groups"),
        P("groups"),
        P(("groups", "ffn"), None, None, None),
        P(),
        P(None, "ffn"),
        P(None, "ffn"),
        P("ffn", None),
    )
    out_specs = P(("groups", "ffn"), None, None, None)
    return jax.shard_map(
        functools.partial(body, ring_is_snake(mesh)),
        mesh=mesh,
        in_specs=in_specs,
        out_specs=out_specs,
        check_vma=False,
    )
```

```python
import functools
import math

import jax
import jax.numpy as jnp
from jax import lax
from jax.experimental import pallas as pl
from jax.experimental.pallas import tpu as pltpu
from jax.sharding import PartitionSpec as P

KVH = 8
CORES = 2

epsilon = 1e-05


def ring_is_snake(mesh):
    row = mesh.devices.reshape(mesh.shape["groups"], mesh.shape["ffn"])[0]
    chips = [getattr(row[i], "coords", None) for i in range(0, len(row), CORES)]
    if len(chips) < 4 or any(c is None for c in chips):
        return False
    return any(
        all(c[axis] == chips[i % 2][axis] for i, c in enumerate(chips))
        and chips[0][axis] != chips[1][axis]
        for axis in range(len(chips[0]))
    )


def layer_kernel(
    ring,
    snake,
    q_hbm,
    bkv_hbm,
    cache_hbm,
    prefix_ref,
    valid_ref,
    resid_hbm,
    gain_hbm,
    wg_hbm,
    wu_hbm,
    wd_hbm,
    out_ref,
    q_ref,
    bkv_ref,
    resid_ref,
    gain_ref,
    cache,
    wg,
    wu,
    wd,
    xg,
    acc_g,
    acc_u,
    sumsq,
    hid,
    csum,
    psend,
    precv,
    rsend,
    rrecv,
    lsend,
    lrecv,
    in_sem,
    cache_sem,
    w_sem,
    ag_recv,
    ag_right,
    ag_left,
    ag_pair,
    ag_pair_recv,
    p_ssem,
    p_rsem,
    r_ssem,
    r_rsem,
    l_ssem,
    l_rsem,
):
    reqs, block_len, width = q_ref.shape
    cache_len = cache.shape[1]
    head_size = cache.shape[2] // 2
    heads = width // head_size
    hidden_here = wg.shape[1]
    model_width = KVH * width
    rows = reqs * block_len
    groups = acc_g.shape[0] // rows
    pieces = xg.shape[1]
    part_width = xg.shape[3]
    parts = pieces // reqs
    part_heads = part_width // head_size
    pairs = KVH // CORES
    half = ring // 2
    paired = snake and ring == 2 * pairs == 8 and groups == 2
    me = lax.axis_index("ffn")
    core = me % CORES
    chip = me // CORES
    if snake:
        here = (1 - chip % 2) * (chip // 2) + (chip % 2) * (ring - 1 - chip // 2)
    else:
        here = chip

    def chip_at(offset):
        place = (here + offset + ring) % ring
        if not snake:
            return place
        back = place // half
        return (1 - back) * (2 * place) + back * (2 * (ring - 1 - place) + 1)

    partner = chip * CORES + (1 - core)
    right = chip_at(1) * CORES + core
    left = chip_at(-1) * CORES + core

    barrier = pltpu.get_barrier_semaphore()
    for other in (partner, right, left):
        pl.semaphore_signal(
            barrier, inc=1, device_id={"ffn": other}, device_id_type=pl.DeviceIdType.MESH
        )

    def cache_copy(r):
        return pltpu.make_async_copy(cache_hbm.at[r], cache.at[r], cache_sem.at[r])

    small_copies = [
        pltpu.make_async_copy(source, target, in_sem.at[n])
        for n, (source, target) in enumerate(
            ((q_hbm, q_ref), (bkv_hbm, bkv_ref), (resid_hbm, resid_ref), (gain_hbm, gain_ref))
        )
    ]
    for copy in small_copies:
        copy.start()
    for r in range(reqs):
        cache_copy(r).start()

    def flipped(bits):
        low = (chip + bits) % 2
        high = (chip // 2 + bits // 2) % 2
        return 2 * high + low

    far_chip = chip_at(half)
    other = 1 - core

    def gate_copy(h):
        span = pl.ds(pl.multiple_of(h * width, width), width)
        return pltpu.make_async_copy(wg_hbm.at[span], wg.at[span], w_sem.at[0, h])

    def up_copy(h):
        span = pl.ds(pl.multiple_of(h * width, width), width)
        return pltpu.make_async_copy(wu_hbm.at[span], wu.at[span], w_sem.at[1, h])

    def down_copy(h):
        span = pl.ds(pl.multiple_of(h * width, width), width)
        return pltpu.make_async_copy(wd_hbm.at[:, span], wd.at[:, span], w_sem.at[2, h])

    def head_at(step):
        return flipped(step // CORES) * CORES + step % CORES if paired else step

    def start_gate_up(step, carry):
        gate_copy(head_at(step)).start()
        up_copy(head_at(step)).start()
        return carry

    def wait_gate_up(step, carry):
        gate_copy(head_at(step)).wait()
        up_copy(head_at(step)).wait()
        return carry

    def start_down(j, carry):
        @pl.when(j < pairs)
        def _():
            down_copy(give_chip(j) * CORES + other).start()

        @pl.when(j > 0)
        def _():
            down_copy(give_chip(j - 1) * CORES + core).start()

        return carry

    def give_chip(j):
        return flipped(pairs - 1 - j) if paired else j

    def send(source, target, ssem, rsem, device):
        return pltpu.make_async_remote_copy(
            src_ref=source,
            dst_ref=target,
            send_sem=ssem,
            recv_sem=rsem,
            device_id={"ffn": device},
            device_id_type=pl.DeviceIdType.MESH,
        )

    def to_right(s, i):
        return send(xg.at[s, i], xg.at[s, i], ag_right.at[s, i], ag_recv.at[s, i], right)

    def to_left(s, i):
        return send(xg.at[s, i], xg.at[s, i], ag_left.at[s, i], ag_recv.at[s, i], left)

    def to_pair(s):
        return send(xg.at[s], xg.at[s], ag_pair.at[s], ag_pair_recv.at[s], partner)

    def goes_right(i):
        return i < pieces // 2

    group = me // KVH
    scale = math.log2(math.e) / (head_size**0.5)
    for copy in small_copies:
        copy.wait()
    for r in range(reqs):
        cache_copy(r).wait()
    lax.fori_loop(0, KVH, start_gate_up, 0)

    def attend(step, carry):
        r = step // parts
        part = step % parts

        columns = pl.ds(pl.multiple_of(part * part_width, part_width), part_width)
        query = q_ref[r, :, columns]
        stacked = jnp.concatenate(
            [query[:, h * head_size : (h + 1) * head_size] for h in range(part_heads)], axis=0
        )
        contract = (((1,), (1,)), ((), ()))
        far = lax.dot_general(
            stacked, cache[r, :, :head_size], contract, preferred_element_type=jnp.float32
        )
        near = lax.dot_general(
            stacked, bkv_ref[r, :, :head_size], contract, preferred_element_type=jnp.float32
        )
        seen = prefix_ref[group * reqs + r]
        live = valid_ref[group * reqs + r]
        far_at = lax.broadcasted_iota(jnp.int32, (1, cache_len), 1)
        near_at = lax.broadcasted_iota(jnp.int32, (1, block_len), 1)
        far = jnp.where(far_at < seen, far, -1e30)
        near = jnp.where(near_at < live, near, -1e30)
        peak = jnp.maximum(
            jnp.max(far, axis=-1, keepdims=True), jnp.max(near, axis=-1, keepdims=True)
        )
        far = jnp.exp2((far - peak) * scale)
        near = jnp.exp2((near - peak) * scale)
        total = jnp.sum(far, axis=-1, keepdims=True) + jnp.sum(near, axis=-1, keepdims=True)
        inverse = 1.0 / total
        mixed = jnp.dot(
            (far * inverse).astype(jnp.bfloat16),
            cache[r, :, head_size:],
            preferred_element_type=jnp.float32,
        ) + jnp.dot(
            (near * inverse).astype(jnp.bfloat16),
            bkv_ref[r, :, head_size:],
            preferred_element_type=jnp.float32,
        )
        side = jnp.concatenate(
            [mixed[h * block_len : (h + 1) * block_len] for h in range(part_heads)], axis=1
        )
        state = resid_ref[r, :, columns].astype(jnp.float32) + side
        xg[me, step] = state.astype(jnp.bfloat16)

        @pl.when(step == 0)
        def _():
            pl.semaphore_wait(barrier, 3)

        to_right(me, step).start()
        to_left(me, step).start()
        return carry

    lax.fori_loop(0, pieces, attend, 0)
    to_pair(me).start()

    def block_of(s):
        return jnp.concatenate(
            [
                jnp.concatenate([xg[s, r * parts + part] for part in range(parts)], axis=1)
                for r in range(reqs)
            ],
            axis=0,
        )

    def fold(square):
        folded = square[:, :head_size]
        for h in range(1, square.shape[1] // head_size):
            folded = folded + square[:, h * head_size : (h + 1) * head_size]
        return folded

    def absorb(s):
        mine = pl.ds(pl.multiple_of((s // KVH) * rows, rows), rows)
        span = pl.ds(pl.multiple_of((s % KVH) * width, width), width)
        block = block_of(s).astype(jnp.float32)
        sumsq[mine] += fold(block * block)
        scaled = (block * gain_ref[:, span]).astype(jnp.bfloat16)
        acc_g[mine] += jnp.dot(scaled, wg[span, :], preferred_element_type=jnp.float32)
        acc_u[mine] += jnp.dot(scaled, wu[span, :], preferred_element_type=jnp.float32)

    def absorb_heads(k):
        span = pl.ds(pl.multiple_of(k * CORES * width, CORES * width), CORES * width)
        block = jnp.concatenate(
            [
                jnp.concatenate(
                    [block_of(g * KVH + k * CORES + c) for c in range(CORES)], axis=1
                )
                for g in range(groups)
            ],
            axis=0,
        ).astype(jnp.float32)
        sumsq[...] += fold(block * block)
        scaled = (block * gain_ref[:, span]).astype(jnp.bfloat16)
        acc_g[...] += jnp.dot(scaled, wg[span, :], preferred_element_type=jnp.float32)
        acc_u[...] += jnp.dot(scaled, wu[span, :], preferred_element_type=jnp.float32)

    def pair_arrived(s):
        to_pair(s).wait_recv()

    def absorb_pair(s):
        pair_arrived(s)
        absorb(s)

    def pass_on(t, last):
        from_left = chip_at(-t) * CORES + core
        from_right = chip_at(t) * CORES + core
        for i in range(pieces):
            to_right(from_left, i).wait_recv()
            if not last or goes_right(i):
                to_right(from_left, i).start()
            to_left(from_right, i).wait_recv()
            if not last or not goes_right(i):
                to_left(from_right, i).start()
        to_pair(from_left).start()
        to_pair(from_right).start()

    def absorb_step(t):
        absorb(chip_at(-t) * CORES + core)
        absorb(chip_at(t) * CORES + core)
        absorb_pair(chip_at(-t) * CORES + 1 - core)
        absorb_pair(chip_at(t) * CORES + 1 - core)

    def from_far():
        for i in range(pieces):
            (to_right if goes_right(i) else to_left)(far_chip * CORES + core, i).wait_recv()
        to_pair(far_chip * CORES + core).start()

    acc_g[...] = jnp.zeros_like(acc_g)
    acc_u[...] = jnp.zeros_like(acc_u)
    sumsq[...] = jnp.zeros_like(sumsq)

    if paired:
        def from_both(t):
            pair_arrived(chip_at(-t) * CORES + other)
            pair_arrived(chip_at(t) * CORES + other)

        pass_on(1, False)
        pair_arrived(partner)
        pass_on(2, False)
        lax.fori_loop(0, pairs + 1, start_down, 0)
        from_both(1)
        from_both(2)

        def stage(j, carry):
            @pl.when(j == 1)
            def _():
                pass_on(3, True)
                from_both(3)

            @pl.when(j == 2)
            def _():
                from_far()

            @pl.when(j == 3)
            def _():
                pair_arrived(far_chip * CORES + other)

            for c in range(CORES):
                wait_gate_up(j * CORES + c, 0)
            absorb_heads(flipped(j))
            return carry

        lax.fori_loop(0, pairs, stage, 0)
    else:
        pass_on(1, half == 2)
        lax.fori_loop(0, pairs + 1, start_down, 0)
        lax.fori_loop(0, KVH, wait_gate_up, 0)
        absorb(me)
        absorb_pair(partner)
        absorb_step(1)

        def middle(t, carry):
            pass_on(t, False)
            absorb_step(t)
            return carry

        if half > 2:
            lax.fori_loop(2, half - 1, middle, 0)
            pass_on(half - 1, True)
            absorb_step(half - 1)
        from_far()
        absorb(far_chip * CORES + core)
        absorb_pair(far_chip * CORES + other)

    mean_square = jnp.sum(sumsq[...], axis=-1, keepdims=True) / model_width
    root = lax.rsqrt(mean_square + epsilon)
    gate = acc_g[...] * root
    up = acc_u[...] * root
    hid[...] = (gate * jax.nn.sigmoid(gate) * up).astype(jnp.bfloat16)

    def pair_copy(k):
        return send(psend.at[k], precv.at[k], p_ssem.at[k], p_rsem.at[k], partner)

    def column_of(k, parity):
        return pl.ds(pl.multiple_of((k * CORES + parity) * width, width), width)

    cuts = []
    for g in range(groups):
        for i in range(pieces):
            top = g * rows + i // parts * block_len
            side = i % parts * part_width
            cuts.append((g, i, (slice(top, top + block_len), slice(side, side + part_width))))

    def give(k):
        down_copy(k * CORES + other).wait()
        share = jnp.dot(hid[...], wd[:, column_of(k, other)], preferred_element_type=jnp.float32)
        for g, i, cut in cuts:
            psend[k, g, i] = share[cut].astype(jnp.bfloat16)
        pair_copy(k).start()

    def keep(k):
        down_copy(k * CORES + core).wait()
        share = jnp.dot(hid[...], wd[:, column_of(k, core)], preferred_element_type=jnp.float32)
        pair_copy(k).wait_recv()
        for g, i, cut in cuts:
            csum[k, g, i] = share[cut] + precv[k, g, i].astype(jnp.float32)

    def right_copy(t, i):
        return send(rsend.at[t, i], rrecv.at[t, i], r_ssem.at[t, i], r_rsem.at[t, i], right)

    def left_copy(t, i):
        return send(lsend.at[t, i], lrecv.at[t, i], l_ssem.at[t, i], l_rsem.at[t, i], left)

    def ring_move(t, i, first, copy_of, out_buf, in_buf, offset):
        target = chip_at(offset)

        def own():
            return csum[target % pairs, target // pairs, i]

        fed = (t < half - 1) | ((t == half - 1) & first)

        @pl.when(fed)
        def _():
            copy_of(t, i).wait_recv()
            total = own() + in_buf[t, i].astype(jnp.float32)
            out_buf[t - 1, i] = total.astype(jnp.bfloat16)

        @pl.when(jnp.logical_not(fed))
        def _():
            out_buf[t - 1, i] = own().astype(jnp.bfloat16)

        copy_of(t - 1, i).start()

    def ring_step(t):
        def piece(i, carry):
            late = i >= pieces // 2

            @pl.when((t < half) | late)
            def _():
                ring_move(t, pieces - 1 - i, late, right_copy, rsend, rrecv, t)
                ring_move(t, i, late, left_copy, lsend, lrecv, -t)

            return carry

        lax.fori_loop(0, pieces, piece, 0)

    if paired:
        def down(j, carry):
            @pl.when(j < pairs)
            def _():
                give(give_chip(j))

            @pl.when((j > 0) & (j <= pairs))
            def _():
                keep(give_chip(j - 1))

            @pl.when((j == 1) | (j > 2))
            def _():
                ring_step(jnp.minimum(half, half + 2 - j))

            return carry

        lax.fori_loop(0, pairs + 2, down, 0)
    else:

        def give_one(j, carry):
            give(j)
            return carry

        def keep_one(j, carry):
            keep(j)
            return carry

        def ring_one(j, carry):
            ring_step(half - j)
            return carry

        lax.fori_loop(0, pairs, give_one, 0)
        lax.fori_loop(0, pairs, keep_one, 0)
        lax.fori_loop(0, half, ring_one, 0)
    for i in range(pieces):
        right_copy(0, i).wait_recv()
        left_copy(0, i).wait_recv()
        value = csum[chip % pairs, chip // pairs, i]
        value = value + rrecv[0, i].astype(jnp.float32) + lrecv[0, i].astype(jnp.float32)
        columns = pl.ds(i % parts * part_width, part_width)
        value = xg[me, i].astype(jnp.float32) + value
        out_ref[i // parts, :, columns] = value.astype(jnp.bfloat16)

    def ring_sent(t, carry):
        for i in range(pieces):
            right_copy(t, i).wait_send()
            left_copy(t, i).wait_send()
        return carry

    lax.fori_loop(0, half - 1, ring_sent, 0)
    for i in range(pieces):
        (right_copy if goes_right(i) else left_copy)(half - 1, i).wait_send()

    def pair_sent(k, carry):
        pair_copy(k).wait_send()
        return carry

    lax.fori_loop(0, pairs, pair_sent, 0)

    def gather_sent(t, carry):
        for i in range(pieces):
            to_right(chip_at(-t) * CORES + core, i).wait_send()
            to_left(chip_at(t) * CORES + core, i).wait_send()
        to_pair(chip_at(-t) * CORES + core).wait_send()
        to_pair(chip_at(t) * CORES + core).wait_send()
        return carry

    for i in range(pieces):
        to_right(me, i).wait_send()
        to_left(me, i).wait_send()
        if goes_right(i):
            to_right(chip_at(1 - half) * CORES + core, i).wait_send()
        else:
            to_left(chip_at(half - 1) * CORES + core, i).wait_send()
    for s in (me, *(chip_at(t) * CORES + core for t in (half, half - 1, 1 - half))):
        to_pair(s).wait_send()
    lax.fori_loop(1, half - 1, gather_sent, 0)


def body(
    snake,
    queries,
    block_kv,
    cache_kv,
    prefix_len,
    block_valid,
    resid,
    norm_gain,
    w_gate,
    w_up,
    w_down,
):
    count = lax.axis_size("ffn")
    ring = count // CORES
    half = ring // 2
    _, reqs, block_len, width = queries.shape
    hidden_here = w_gate.shape[1]
    groups = count // KVH
    rows = reqs * block_len
    pairs = KVH // CORES
    lanes = block_kv.shape[3] // 2
    parts = 2 if (width // lanes) % 2 == 0 else 1
    pieces, part_width = reqs * parts, width // parts
    bf16, f32 = jnp.bfloat16, jnp.float32
    vmem = pl.BlockSpec(memory_space=pltpu.VMEM)
    smem = pl.BlockSpec(memory_space=pltpu.SMEM)
    hbm = pl.BlockSpec(memory_space=pl.ANY)
    dma = pltpu.SemaphoreType.DMA
    flops = 2 * groups * rows * KVH * width * hidden_here * 3
    out = pl.pallas_call(
        functools.partial(layer_kernel, ring, snake),
        out_shape=jax.ShapeDtypeStruct((reqs, block_len, width), bf16),
        in_specs=[hbm, hbm, hbm, smem, smem, hbm, hbm, hbm, hbm, hbm],
        out_specs=vmem,
        scratch_shapes=[
            pltpu.VMEM(queries.shape[1:], bf16),
            pltpu.VMEM(block_kv.shape[1:], bf16),
            pltpu.VMEM(resid.shape[1:], bf16),
            pltpu.VMEM((1, norm_gain.shape[0]), f32),
            pltpu.VMEM(cache_kv.shape[1:], bf16),
            pltpu.VMEM(w_gate.shape, bf16),
            pltpu.VMEM(w_up.shape, bf16),
            pltpu.VMEM(w_down.shape, bf16),
            pltpu.VMEM((count, pieces, block_len, part_width), bf16),
            pltpu.VMEM((groups * rows, hidden_here), f32),
            pltpu.VMEM((groups * rows, hidden_here), f32),
            pltpu.VMEM((groups * rows, lanes), f32),
            pltpu.VMEM((groups * rows, hidden_here), bf16),
            pltpu.VMEM((pairs, groups, pieces, block_len, part_width), f32),
            pltpu.VMEM((pairs, groups, pieces, block_len, part_width), bf16),
            pltpu.VMEM((pairs, groups, pieces, block_len, part_width), bf16),
            pltpu.VMEM((half, pieces, block_len, part_width), bf16),
            pltpu.VMEM((half, pieces, block_len, part_width), bf16),
            pltpu.VMEM((half, pieces, block_len, part_width), bf16),
            pltpu.VMEM((half, pieces, block_len, part_width), bf16),
            dma((4,)),
            dma((reqs,)),
            dma((3, KVH)),
            dma((count, pieces)),
            dma((count, pieces)),
            dma((count, pieces)),
            dma((count,)),
            dma((count,)),
            dma((pairs,)),
            dma((pairs,)),
            dma((half, pieces)),
            dma((half, pieces)),
            dma((half, pieces)),
            dma((half, pieces)),
        ],
        compiler_params=pltpu.CompilerParams(
            collective_id=0, has_side_effects=True, vmem_limit_bytes=57 * 1024 * 1024
        ),
        cost_estimate=pl.CostEstimate(
            flops=flops, bytes_accessed=6 * KVH * width * hidden_here, transcendentals=0
        ),
    )(
        queries[0],
        block_kv[0],
        cache_kv[0],
        prefix_len,
        block_valid,
        resid[0],
        norm_gain.reshape(1, -1),
        w_gate,
        w_up,
        w_down,
    )
    return out[None]


def solution(mesh):
    in_specs = (
        P(("groups", "ffn"), None, None, None),
        P(("groups", "ffn"), None, None, None),
        P(("groups", "ffn"), None, None, None),
        P("groups"),
        P("groups"),
        P(("groups", "ffn"), None, None, None),
        P(),
        P(None, "ffn"),
        P(None, "ffn"),
        P("ffn", None),
    )
    out_specs = P(("groups", "ffn"), None, None, None)
    return jax.shard_map(
        functools.partial(body, ring_is_snake(mesh)),
        mesh=mesh,
        in_specs=in_specs,
        out_specs=out_specs,
        check_vma=False,
    )
```
